128 devices in a mesh: ctx: 8 (over z, core), exp: 16 (over y, x).
Axes of the slice: x: 4, y: 4, z: 4, core: 2. Of those that a mesh axis runs over, the one named last changes fastest.
Arguments:
- mixer_input: bfloat16 [1024, 8192], P('ctx', 'exp'), may hold values from -6 to 6
- mixer_gate: bfloat16 [1024, 8192], P('ctx', 'exp'), may hold values from -6 to 6
- step_size: bfloat16 [1024, 8192], P('ctx', 'exp'), may hold values from 0.002 to 25
- write_coeffs: float32 [1024, 16], P('ctx'), may hold values from -1.5 to 1.5
- read_coeffs: float32 [1024, 16], P('ctx'), may hold values from -1.5 to 1.5
- decay_rates: float32 [8192, 16], P('exp'), may hold values from 0.01 to 0.6
- skip_scale: float32 [8192], P('exp'), may hold values from 0.5 to 1.5
- out_weight: bfloat16 [8192, 4096], P('exp', 'ctx'), may hold values from -0.0625 to 0.0625
- residual_in: bfloat16 [1024, 4096], P(('ctx', 'exp')), may hold values from -6 to 6
- norm_gain: float32 [4096], replicated, may hold values from 0.1 to 1.9
- expert_ids: int32 [1024, 2], P(('ctx', 'exp')), may hold values from 0 to 15, all different within a row; in each aligned block of 8 rows (0 to 7, 8 to 15, ...) at most 2 rows name the same one
- gate_weights: bfloat16 [1024, 2], P(('ctx', 'exp')), may hold values from 0.049804688 to 1
- up_weight: bfloat16 [16, 4096, 12288], P('exp', None, 'ctx'), may hold values from -0.09375 to 0.09375
- down_weight: bfloat16 [16, 12288, 4096], P('exp', 'ctx'), may hold values from -0.0546875 to 0.0546875
Outputs:
- layer_out: bfloat16 [1024, 4096], P(('ctx', 'exp'))
The draws below stay inside these ranges and needn't reach their ends.
Inputs may be any that keep to these rules, and one draw needn't show every extreme that they name: `expert_ids`: each row names 2 different experts; among the 8 rows of one device no expert is named more than 2 times.
All inputs are finite; a program needn't handle non-finite values.
Results may differ from the reference program's by a relative error of at most 0.0057.
Values may be sent and summed in bfloat16 or wider, within the bound.
A program may use at most 128 MiB of HBM per device.

```python
import math
import jax
import jax.numpy as jnp
import numpy as np
from jax import lax

D = 4096
MIXER_CHANNELS = 8192
NS = 16
FF = 12288
TOP = 2
TOK_DEV = 8
EXPERTS = 16
CAP = 2
PROMPT_TOKENS = 1024


def quick_channels(key, share_permille):
    return jax.random.randint(key, (MIXER_CHANNELS,), 0, 1000) < share_permille


def scatter_sample(key, shape, low_value, high_value):
    uniform_draw = jax.random.uniform(key, shape, jnp.float32)
    return jnp.exp(math.log(low_value) + uniform_draw * math.log(high_value / low_value))


def draw_decay_rates(key, part):
    share_permille = 500
    quick_mask = quick_channels(key, share_permille)
    key = jax.random.fold_in(key, 11)
    quick_rates = scatter_sample(key, (MIXER_CHANNELS, NS), 0.15, 0.6)
    slow_rates = 0.02 * scatter_sample(jax.random.fold_in(key, 1), (MIXER_CHANNELS, NS), 0.7, 1.4)
    return jnp.where(quick_mask[:, None], quick_rates, slow_rates)


def draw_step_size(key, part):
    share_permille = 500
    quick_mask = quick_channels(key, share_permille)
    key = jax.random.fold_in(key, 12)
    first_key, random_key_two, random_key_three = jax.random.split(key, 3)
    quick_steps = scatter_sample(first_key, (PROMPT_TOKENS, MIXER_CHANNELS), 0.05, 0.2)
    gentle_step_sizes = 12.5 / PROMPT_TOKENS * scatter_sample(jax.random.fold_in(first_key, 1), (PROMPT_TOKENS, MIXER_CHANNELS), 0.5, 2.0)
    sudden_positions = jax.random.randint(random_key_two, (2,), 0, PROMPT_TOKENS)
    sudden_mask = jnp.any(jnp.arange(PROMPT_TOKENS)[:, None] == sudden_positions[None, :], axis=1)
    sudden_step_sizes = scatter_sample(random_key_three, (PROMPT_TOKENS, MIXER_CHANNELS), 11.0, 25.0)
    gentle_everywhere = jnp.where(sudden_mask[:, None], sudden_step_sizes, gentle_step_sizes)
    return jnp.where(quick_mask[None, :], quick_steps, gentle_everywhere).astype(jnp.bfloat16)


def levels(key, extent, cuts, low, high):
    loudness = 1.0
    for dim, parts in cuts:
        heights = jax.random.uniform(jax.random.fold_in(jax.random.fold_in(key, 6), dim), (parts,), jnp.float32, low / len(cuts), high / len(cuts))
        loudness = loudness * jnp.repeat(jnp.exp(heights), extent[dim] // parts).reshape((-1,) + (1,) * (len(extent) - 1 - dim))
    return loudness


def deal_out(key, own, number, rows, count, top, reach, slope):
    sequence = jax.random.permutation(key, count)
    heavy_load, ordinary = load_shares(count, rows * top, reach, slope, True), load_shares(count, rows * top, reach, slope, False)
    places = jnp.arange(count)

    def named(lengths, turn):
        used = int((lengths > 0).sum())
        fixed = max(1, used // 4)
        moved = fixed + (places - fixed + turn * (used - fixed)) % max(1, count - fixed)
        return jnp.zeros((count,), jnp.int32).at[sequence[jnp.where(places < fixed, places, moved)]].set(jnp.asarray(lengths, jnp.int32))

    lengths = jnp.where(number % 4 == 0, named(heavy_load, number // 4), named(ordinary, number - number // 4 - 1))
    mixed = jax.random.permutation(jax.random.fold_in(own, 3), count)
    source_of, receiver = mixed[0:count // 2 * 2:2], mixed[1:count // 2 * 2:2]
    margin = jnp.minimum(lengths[source_of] - 1, reach - lengths[receiver]) // 2
    margin = jnp.where((source_of == sequence[0]) | (receiver == sequence[0]) | (lengths[receiver] == 0), 0, jnp.maximum(margin, 0))
    moved = jax.random.randint(jax.random.fold_in(own, 4), (count // 2,), 0, 1 << 20) % (margin + 1)
    lengths = lengths.at[source_of].add(-moved).at[receiver].add(moved)
    labels = jnp.searchsorted(jnp.cumsum(lengths), jnp.arange(rows * top), side="right").astype(jnp.int32)
    grid = labels.reshape(top, rows).T
    grid = grid[jax.random.permutation(jax.random.fold_in(own, 1), rows)]
    turn = jax.random.randint(jax.random.fold_in(own, 2), (rows, 1), 0, top)
    return jnp.take_along_axis(grid, (jnp.arange(top)[None, :] + turn) % top, axis=1)


def load_shares(number_of, total, limit, lean, full):
    portions = [(1 << 20) // math.isqrt(standing ** lean) + 1 for standing in range(1, number_of + 1)]
    largest = limit if full else min(limit, max(-(-total // number_of), total * portions[0] // sum(portions)))
    least = 1 if total - largest >= number_of - 1 else 0
    holding, surplus = [largest] + [least] * (number_of - 1), total - largest - least * (number_of - 1)
    while surplus > 0:
        free = [i for i in range(1, number_of) if holding[i] < largest] or [i for i in range(1, number_of) if holding[i] < limit]
        pool, remaining = sum([portions[i] for i in free]), surplus
        for i in free:
            extra = min(limit - holding[i], max(1, remaining * portions[i] // pool), surplus)
            holding[i] = holding[i] + extra
            surplus = surplus - extra
    return np.array(holding)


def centred(stream_key, extent, scale, bound, shards=(), kind=jnp.bfloat16):
    factor_of = levels(stream_key, extent, shards, -0.22, 0.18) if shards else 1.0
    values = jax.random.normal(stream_key, extent, jnp.float32) * scale * factor_of
    return jnp.minimum(jnp.maximum(values, -bound), bound).astype(kind)


def setup_inputs(seed: int = 0) -> dict:
    key_list = jax.random.split(jax.random.key(seed), 15)
    mixer_input = centred(key_list[0], (PROMPT_TOKENS, MIXER_CHANNELS), 1.0, 6.0, ((0, 8), (1, 16)))
    mixer_gate = centred(key_list[1], (PROMPT_TOKENS, MIXER_CHANNELS), 1.0, 6.0, ((0, 8), (1, 16)))
    step_size = draw_step_size(jax.random.fold_in(key_list[14], 71), 0)
    write_coeffs = centred(key_list[3], (PROMPT_TOKENS, NS), 0.25, 1.5, ((0, 8),), jnp.float32)
    read_coeffs = centred(key_list[4], (PROMPT_TOKENS, NS), 0.25, 1.5, ((0, 8),), jnp.float32)
    decay_rates = draw_decay_rates(jax.random.fold_in(key_list[14], 71), 0)
    skip_scale = jnp.clip(0.5 + 1.0 * jax.random.uniform(key_list[6], (MIXER_CHANNELS,), jnp.float32) ** levels(key_list[6], (MIXER_CHANNELS,), ((0, 16),), -0.2, 0.2), 0.5, 1.5)
    out_weight = centred(key_list[7], (MIXER_CHANNELS, D), MIXER_CHANNELS ** -0.5, 0.0625, ((0, 16), (1, 8)))
    residual_in = centred(key_list[8], (PROMPT_TOKENS, D), 1.0, 6.0, ((0, 128),))
    norm_gain = jnp.clip(1.0 + 0.18 * jax.random.normal(key_list[9], (D,), jnp.float32), 0.1, 1.9)
    expert_ids_keys = jax.random.split(jax.random.fold_in(key_list[10], 1), PROMPT_TOKENS // TOK_DEV)
    expert_ids_turns = jax.random.permutation(jax.random.fold_in(key_list[10], 3), PROMPT_TOKENS // TOK_DEV)
    expert_ids = jax.vmap(lambda own, number: deal_out(jax.random.fold_in(key_list[10], 2), own, number, TOK_DEV, EXPERTS, TOP, CAP, 2))(expert_ids_keys, expert_ids_turns).reshape((PROMPT_TOKENS, TOP))
    gate_weights = jnp.clip(0.049804688 + 0.9501953 * jax.random.uniform(key_list[11], (PROMPT_TOKENS, TOP), jnp.float32) ** levels(key_list[11], (PROMPT_TOKENS, TOP), ((0, 128),), -0.2, 0.2), 0.049804688, 1.0).astype(jnp.bfloat16)
    up_weight = centred(key_list[12], (EXPERTS, D, FF), D ** -0.5, 0.09375, ((0, 16), (2, 8)))
    down_weight = centred(key_list[13], (EXPERTS, FF, D), FF ** -0.5, 0.0546875, ((0, 16), (1, 8)))
    return {"mixer_input": mixer_input, "mixer_gate": mixer_gate, "step_size": step_size, "write_coeffs": write_coeffs, "read_coeffs": read_coeffs, "decay_rates": decay_rates, "skip_scale": skip_scale, "out_weight": out_weight, "residual_in": residual_in, "norm_gain": norm_gain, "expert_ids": expert_ids, "gate_weights": gate_weights, "up_weight": up_weight, "down_weight": down_weight}


EPSILON = 1e-05

def combine_pairs(earlier, later):
    return (earlier[0] * later[0], later[0] * earlier[1] + later[1])

def reference(mixer_input, mixer_gate, step_size, write_coeffs, read_coeffs, decay_rates, skip_scale, out_weight, residual_in, norm_gain, expert_ids, gate_weights, up_weight, down_weight):
    block_width = math.gcd(MIXER_CHANNELS, 512)
    block_total = MIXER_CHANNELS // block_width

    def by_blocks(source):
        return source.reshape(PROMPT_TOKENS, block_total, block_width).transpose(1, 0, 2)

    def mixer_block(operands):
        block_input, block_gate, block_step, block_rates, block_skip = operands
        step_wide = block_step.astype(jnp.float32)
        input_wide = block_input.astype(jnp.float32)
        decays = jnp.exp(-(step_wide[:, :, None] * block_rates[None, :, :]))
        pushes = (step_wide * input_wide)[:, :, None] * write_coeffs[:, None, :]
        reached, states = lax.associative_scan(combine_pairs, (decays, pushes), axis=0)
        readout = lax.optimization_barrier(jnp.sum(states * read_coeffs[:, None, :], axis=2)) + block_skip[None, :] * input_wide
        return (readout * jax.nn.silu(block_gate.astype(jnp.float32))).astype(jnp.bfloat16)
    mixed_blocks = lax.map(mixer_block, (by_blocks(mixer_input), by_blocks(mixer_gate), by_blocks(step_size), decay_rates.reshape(block_total, block_width, NS), skip_scale.reshape(block_total, block_width)))
    mixed = mixed_blocks.transpose(1, 0, 2).reshape(PROMPT_TOKENS, MIXER_CHANNELS)
    mixer_sum = jnp.dot(mixed, out_weight, preferred_element_type=jnp.float32)
    stream = (residual_in.astype(jnp.float32) + mixer_sum).astype(jnp.bfloat16)
    stream_wide = stream.astype(jnp.float32)
    normed = (stream_wide * lax.rsqrt(lax.optimization_barrier(jnp.mean(stream_wide * stream_wide, axis=1, keepdims=True)) + EPSILON) * norm_gain[None, :]).astype(jnp.bfloat16)
    pair_experts = expert_ids.reshape(-1).astype(jnp.int32)
    pair_gates = gate_weights.reshape(-1).astype(jnp.float32)
    slot_limit = PROMPT_TOKENS // TOK_DEV * CAP

    def single_expert(expert):
        matches = pair_experts == expert
        chosen = jnp.nonzero(matches, size=slot_limit, fill_value=0)[0].astype(jnp.int32)
        is_valid = (jnp.arange(slot_limit, dtype=jnp.int32) < jnp.sum(matches.astype(jnp.int32))).astype(jnp.float32)
        tokens_in = normed[chosen // TOP]
        lifted = jax.nn.silu(jnp.dot(tokens_in, up_weight[expert], preferred_element_type=jnp.float32)).astype(jnp.bfloat16)
        lowered = jnp.dot(lifted, down_weight[expert], preferred_element_type=jnp.float32)
        weighted = (lowered * (pair_gates[chosen] * is_valid)[:, None]).astype(jnp.bfloat16)
        return (chosen, weighted)
    chosen_all, weighted_all = lax.map(single_expert, jnp.arange(EXPERTS, dtype=jnp.int32))
    pair_sums = jnp.zeros((PROMPT_TOKENS * TOP, D), jnp.float32).at[chosen_all.reshape(-1)].add(weighted_all.reshape(-1, D).astype(jnp.float32))
    token_sums = lax.optimization_barrier(jnp.sum(pair_sums.reshape(PROMPT_TOKENS, TOP, D), axis=1))
    return (stream_wide + token_sums).astype(jnp.bfloat16)
```

```python
import functools
import math

import jax
import jax.numpy as jnp
from jax import lax
from jax.experimental import pallas as pl
from jax.experimental.pallas import tpu as pltpu
from jax.sharding import PartitionSpec as P

MESH = pl.DeviceIdType.MESH
CAP = 2
EPSILON = 1e-05
LOG2E = math.log2(math.e)
F32 = jnp.float32
BF16 = jnp.bfloat16
STEPS = 16


def remote(src, dst, send_sem, recv_sem, device):
    return pltpu.make_async_remote_copy(
        src_ref=src,
        dst_ref=dst,
        send_sem=send_sem,
        recv_sem=recv_sem,
        device_id=device,
        device_id_type=MESH,
    )


def loop(count, body):
    def step(k, carry):
        body(k)
        return carry

    lax.fori_loop(0, count, step, 0)


def kernel(
    nctx,
    nexp,
    x_hbm,
    gate_hbm,
    step_hbm,
    write_hbm,
    read_hbm,
    rates_hbm,
    skip_hbm,
    ow_hbm,
    res_hbm,
    gain_hbm,
    ids_hbm,
    pairgate_hbm,
    up_hbm,
    down_hbm,
    out_ref,
    x_v,
    gate_v,
    step_v,
    write_v,
    read_v,
    rates_v,
    skip_v,
    res_v,
    gain_v,
    ids_v,
    pairgate_v,
    write_t,
    read_t,
    up_v,
    down_v,
    w_v,
    dt_f,
    u_f,
    wb_v,
    rb_v,
    rate2_v,
    h_v,
    hsend,
    hrecv,
    mixed_v,
    psend,
    precv,
    zsend,
    zrecv,
    stream_v,
    table_v,
    dsend,
    drecv,
    rows_v,
    acc_v,
    lifted_v,
    osend,
    orecv,
    okeep,
    rsend,
    rrecv,
    bsend,
    brecv,
    lsem,
    wsem,
    wswap,
    hs_sem,
    hr_sem,
    ms_sem,
    mr_sem,
    ps_sem,
    pr_sem,
    zs_sem,
    zr_sem,
    ds_sem,
    dr_sem,
    xs_sem,
    xr_sem,
    fs_sem,
    fr_sem,
    os_sem,
    or_sem,
    rs_sem,
    rr_sem,
    bs_sem,
    br_sem,
):
    i = lax.axis_index("ctx")
    j = lax.axis_index("exp")
    nz = nctx // 2
    z = lax.div(i, 2)
    c = lax.rem(i, 2)
    partner = (z * 2 + 1 - c, j)
    tokens, channels = x_hbm.shape
    states = write_hbm.shape[0]
    mine, width = res_hbm.shape
    block = width // nctx
    hidden = up_hbm.shape[1]
    chunks = nctx
    slots = nexp * CAP
    half = nz * slots

    def at_z(zz):
        return (zz * 2 + c, j)

    def at_e(e):
        return (i, e)

    def z_next(k):
        return lax.rem(z + k, nz)

    def e_next(k):
        return lax.rem(j + k, nexp)

    small = [
        (write_hbm, write_v),
        (read_hbm, read_v),
        (rates_hbm, rates_v),
        (step_hbm, step_v),
        (x_hbm, x_v),
        (gate_hbm, gate_v),
        (skip_hbm, skip_v),
        (res_hbm, res_v),
        (gain_hbm, gain_v),
        (ids_hbm, ids_v),
        (pairgate_hbm, pairgate_v),
        (ow_hbm, w_v.at[c]),
    ]
    small = [
        pltpu.make_async_copy(src, dst, lsem.at[n]) for n, (src, dst) in enumerate(small)
    ]
    for copy in small:
        copy.start()

    barrier = pltpu.get_barrier_semaphore()

    def greet_ctx(k):
        pl.semaphore_signal(
            barrier, inc=1, device_id=(lax.rem(i + k + 1, nctx), j), device_id_type=MESH
        )

    def greet_exp(k):
        pl.semaphore_signal(barrier, inc=1, device_id=at_e(e_next(k + 1)), device_id_type=MESH)

    loop(nctx - 1, greet_ctx)
    loop(nexp - 1, greet_exp)

    def up_copy(k):
        part = pl.ds(pl.multiple_of(k * block, block), block)
        return pltpu.make_async_copy(up_hbm.at[part], up_v.at[part], wsem.at[0, k])

    depth = hidden // chunks

    def down_copy(k):
        part = pl.ds(pl.multiple_of(k * depth, depth), depth)
        return pltpu.make_async_copy(down_hbm.at[part], down_v.at[part], wsem.at[1, k])

    loop(chunks, lambda k: up_copy(k).start())
    loop(chunks, lambda k: down_copy(k).start())

    small[0].wait()
    small[1].wait()
    write_t[...] = write_v[...].T
    read_t[...] = read_v[...].T
    diagonal = lax.broadcasted_iota(jnp.int32, (1, states, states), 1) == lax.broadcasted_iota(
        jnp.int32, (1, states, states), 2
    )

    def spread(n):
        part = pl.ds(pl.multiple_of(n * STEPS, STEPS), STEPS)
        for source, wide in ((write_t, wb_v), (read_t, rb_v)):
            rows = jnp.broadcast_to(source[part, :][:, None, :], (STEPS, states, states))
            picked = jnp.sum(jnp.where(diagonal, rows, 0.0), axis=2, keepdims=True)
            wide[part] = jnp.broadcast_to(picked, (STEPS, states, 128))

    loop(tokens // STEPS, spread)
    small[2].wait()
    rate2_v[...] = rates_v[...] * (-LOG2E)
    small[3].wait()
    small[4].wait()

    def widen(n):
        part = pl.ds(pl.multiple_of(n * STEPS, STEPS), STEPS)
        steps = step_v[part, :].astype(F32)
        dt_f[part, :] = steps
        u_f[part, :] = steps * x_v[part, :].astype(F32)

    loop(tokens // STEPS, widen)
    copies = channels // 128

    def advance(h, t, rate2):
        decay = jnp.exp2(dt_f[pl.ds(t, 1), :] * rate2)
        push = u_f[pl.ds(t, 1), :] * jnp.concatenate([wb_v[t]] * copies, axis=1)
        return decay * h + push

    def first(n, carry):
        h, total = carry
        rate2 = rate2_v[...]
        for r in range(STEPS):
            h = advance(h, n * STEPS + r, rate2)
        part = pl.ds(pl.multiple_of(n * STEPS, STEPS), STEPS)
        return h, total + jnp.sum(dt_f[part, :], axis=0, keepdims=True)

    h, total = lax.fori_loop(
        0,
        tokens // STEPS,
        first,
        (jnp.zeros((states, channels), F32), jnp.zeros((1, channels), F32)),
    )
    hsend[0:states, :] = h
    hsend[states : states + 8, :] = jnp.broadcast_to(total, (8, channels))

    pl.semaphore_wait(barrier, nctx + nexp - 2)

    def state_copy(k):
        return remote(
            hsend, hrecv.at[i], hs_sem.at[k], hr_sem.at[i], (lax.rem(i + k, nctx), j)
        )

    for k in range(1, nctx):

        @pl.when(i + k < nctx)
        def _():
            state_copy(k).start()

    small[11].wait()
    swap = remote(w_v.at[c], w_v.at[c], wswap.at[0], wswap.at[1], partner)
    swap.start()

    h_v[...] = jnp.zeros_like(h_v)
    for k in range(nctx - 1):

        @pl.when(k < i)
        def _():
            remote(hsend, hrecv.at[k], hs_sem.at[0], hr_sem.at[k], partner).wait_recv()
            gone = jnp.exp2(rate2_v[...] * hrecv[k, states : states + 1, :])
            h_v[...] = gone * h_v[...] + hrecv[k, 0:states, :]

    small[5].wait()
    small[6].wait()

    def second(n, h):
        part = pl.ds(pl.multiple_of(n * STEPS, STEPS), STEPS)
        rate2 = rate2_v[...]
        reads = []
        for r in range(STEPS):
            t = n * STEPS + r
            h = advance(h, t, rate2)
            seen = h * jnp.concatenate([rb_v[t]] * copies, axis=1)
            reads.append(jnp.sum(seen, axis=0, keepdims=True))
        readout = jnp.concatenate(reads, axis=0)
        readout = readout + skip_v[...] * x_v[part, :].astype(F32)
        gate = gate_v[part, :].astype(F32)
        mixed_v[z, part, :] = (readout * (gate / (1.0 + jnp.exp(-gate)))).astype(BF16)
        return h

    lax.fori_loop(0, tokens // STEPS, second, h_v[...])

    def mixed_copy(k):
        return remote(
            mixed_v.at[z], mixed_v.at[z], ms_sem.at[k], mr_sem.at[z], at_z(z_next(k))
        )

    for k in range(1, nz):
        mixed_copy(k).start()

    pair_rows = 2 * mine

    def psum_copy(zz, k):
        part = pl.ds(pl.multiple_of(zz * pair_rows, pair_rows), pair_rows)
        e = e_next(k)
        return remote(
            psend.at[e, part],
            precv.at[j, part],
            ps_sem.at[zz, k],
            pr_sem.at[zz, j],
            at_e(e),
        )

    swap.wait_recv()

    def project(k):
        zz = z_next(k)

        @pl.when(k > 0)
        def _():
            remote(
                mixed_v.at[zz], mixed_v.at[zz], ms_sem.at[0], mr_sem.at[zz], partner
            ).wait_recv()

        part = pl.ds(pl.multiple_of(zz * pair_rows, pair_rows), pair_rows)
        sides = [
            jnp.dot(mixed_v[zz], w_v[side], preferred_element_type=F32).reshape(nexp, mine, block)
            for side in range(2)
        ]
        psend[:, part, :] = jnp.concatenate(sides, axis=1).astype(BF16)
        loop(nexp - 1, lambda e: psum_copy(zz, e + 1).start())

    loop(nz, project)

    total_rows = nz * pair_rows

    def gather_sum(k, total):
        e = e_next(k)

        def arrive(zz):
            part = pl.ds(pl.multiple_of(zz * pair_rows, pair_rows), pair_rows)
            remote(
                psend.at[e, part], precv.at[e, part], ps_sem.at[zz, 0], pr_sem.at[zz, e], partner
            ).wait_recv()

        loop(nz, arrive)
        return total + precv[e].astype(F32)

    sums = lax.fori_loop(1, nexp, gather_sum, psend[j].astype(F32))
    zsend[...] = sums.reshape(nz, pair_rows, block)
    zrecv[z] = zsend[z]

    def zsum_copy(k):
        zz = z_next(k)
        return remote(zsend.at[zz], zrecv.at[z], zs_sem.at[k], zr_sem.at[z], at_z(zz))

    for k in range(1, nz):
        zsum_copy(k).start()

    for n in (7, 8, 9, 10):
        small[n].wait()
    lanes = lax.broadcasted_iota(jnp.int32, (mine, 128), 1)
    square = lax.broadcasted_iota(jnp.int32, (mine, mine), 0) == lax.broadcasted_iota(
        jnp.int32, (mine, mine), 1
    )

    def column_of(row):
        return jnp.sum(jnp.where(square, row.astype(F32), 0.0), axis=1, keepdims=True)

    first_id = column_of(ids_v[0:1, :]).astype(jnp.int32)
    second_id = column_of(ids_v[1:2, :]).astype(jnp.int32)
    first_hot = (lanes == first_id).astype(F32)
    second_hot = (lanes == second_id).astype(F32)
    earlier = (
        lax.broadcasted_iota(jnp.int32, (mine, mine), 0)
        > lax.broadcasted_iota(jnp.int32, (mine, mine), 1)
    ).astype(F32)
    before = jnp.dot(earlier, first_hot + second_hot, preferred_element_type=F32)
    stacked = chunks * mine
    places = nexp * chunks * CAP
    column = lax.broadcasted_iota(jnp.int32, (stacked, places), 1)
    row = lax.broadcasted_iota(jnp.int32, (stacked, places), 0)
    column_slot = lax.div(column, chunks * CAP) * CAP + lax.rem(column, CAP)
    same_block = lax.rem(lax.div(column, CAP), chunks) == lax.div(row, mine)
    table = jnp.zeros((stacked, places), F32)
    gated = jnp.zeros((stacked, places), F32)
    pair_gates = pairgate_v[...].astype(F32)
    for choice, (ident, hot) in enumerate(((first_id, first_hot), (second_id, second_hot))):
        rank = jnp.sum(before * hot, axis=1, keepdims=True).astype(jnp.int32)
        slot = jnp.concatenate([ident * CAP + rank] * chunks, axis=0)
        taken = jnp.where(same_block & (column_slot == slot), 1.0, 0.0)
        weight = jnp.concatenate([column_of(pair_gates[choice : choice + 1, :])] * chunks, axis=0)
        table = table + taken
        gated = gated + taken * weight
    table_v[...] = gated.astype(BF16)
    table_down = table.T.astype(BF16)

    for k in range(1, nz):
        zz = z_next(k)
        remote(zsend.at[zz], zrecv.at[zz], zs_sem.at[0], zr_sem.at[zz], partner).wait_recv()

    def stack(wide):
        return jnp.concatenate(
            [wide[:, k * block : (k + 1) * block] for k in range(chunks)], axis=0
        )

    res = stack(res_v[...].astype(F32))
    gain = stack(jnp.broadcast_to(gain_v[...], (mine, width)))
    stream = (res + zrecv[...].reshape(stacked, block)).astype(BF16).astype(F32)
    stream_v[...] = stream
    squares = jnp.sum(stream * stream, axis=1, keepdims=True).reshape(chunks, mine, 1)
    scale = lax.rsqrt(jnp.sum(squares, axis=0) / width + EPSILON)
    normed = (stream * jnp.concatenate([scale] * chunks, axis=0) * gain).astype(BF16)

    pack = chunks * CAP
    dsend[...] = (
        jnp.dot(table_down, normed, preferred_element_type=F32)
        .astype(BF16)
        .reshape(nexp, pack, block)
    )

    def dispatch_copy(k):
        e = e_next(k)
        return remote(dsend.at[e], drecv.at[j], ds_sem.at[k], dr_sem.at[j], at_e(e))

    loop(nexp - 1, lambda k: dispatch_copy(k + 1).start())
    drecv[j] = dsend[j]
    source = lax.broadcasted_iota(jnp.int32, (places, places), 1)
    target = lax.broadcasted_iota(jnp.int32, (places, places), 0)
    place = lax.rem(source, CAP)
    chunk_of = lax.rem(lax.div(source, CAP), chunks)
    from_device = lax.div(source, pack)
    order = (chunk_of * slots + from_device * CAP + place == target).astype(F32).astype(BF16)

    def dispatch_arrive(k):
        e = e_next(k + 1)
        remote(dsend.at[e], drecv.at[e], ds_sem.at[0], dr_sem.at[e], partner).wait_recv()

    loop(nexp - 1, dispatch_arrive)
    arranged = jnp.dot(order, drecv[...].reshape(places, block), preferred_element_type=F32)
    own = pl.ds(pl.multiple_of(z * slots, slots), slots)
    rows_v[:, own, :] = arranged.astype(BF16).reshape(chunks, slots, block)

    def rows_part(zz):
        return pl.ds(pl.multiple_of(zz * slots, slots), slots)

    def far_part(zz):
        return pl.ds(pl.multiple_of(half + zz * slots, slots), slots)

    def rows_copy(k, n):
        return remote(
            rows_v.at[k, own],
            rows_v.at[k, own],
            xs_sem.at[k, n],
            xr_sem.at[k, z],
            at_z(z_next(n)),
        )

    def forward_copy(k, zz):
        return remote(
            rows_v.at[k, rows_part(zz)],
            rows_v.at[k, far_part(zz)],
            fs_sem.at[k, zz],
            fr_sem.at[k, zz],
            partner,
        )

    def rows_out(k):
        for n in range(1, nz):
            rows_copy(k, n).start()
        forward_copy(k, z).start()

    loop(chunks, rows_out)

    def rows_arrive(k):
        for n in range(1, nz):
            zz = z_next(n)
            part = rows_part(zz)
            remote(
                rows_v.at[k, part], rows_v.at[k, part], xs_sem.at[k, 0], xr_sem.at[k, zz], partner
            ).wait_recv()
            forward_copy(k, zz).start()

    tile = 512 if hidden % 512 == 0 else hidden
    tiles = hidden // tile

    def lift(k):
        for zz in range(nz):
            forward_copy(k, zz).wait_recv()
        up_copy(k).wait()
        part = pl.ds(pl.multiple_of(k * block, block), block)

        def one(n):
            columns = pl.ds(pl.multiple_of(n * tile, tile), tile)
            product = jnp.dot(rows_v[k], up_v[part, columns], preferred_element_type=F32)

            @pl.when(k == 0)
            def _():
                acc_v[:, columns] = product

            @pl.when(k > 0)
            def _():
                acc_v[:, columns] += product

        loop(tiles, one)

    rows_arrive(0)

    def up_step(k):
        rows_arrive(k + 1)
        lift(k)

    loop(chunks - 1, up_step)
    lift(chunks - 1)

    def activate(n):
        columns = pl.ds(pl.multiple_of(n * tile, tile), tile)
        lifted = acc_v[:, columns]
        lifted_v[:, columns] = (lifted / (1.0 + jnp.exp(-lifted))).astype(BF16)

    loop(tiles, activate)
    loop(chunks, lambda k: down_copy(k).wait())

    def pair_copy(k):
        return remote(osend.at[k], orecv.at[k], os_sem.at[k], or_sem.at[k], partner)

    def back_copy(k, n):
        zz = z_next(n)
        return remote(
            rsend.at[k, zz], rrecv.at[k, z], rs_sem.at[k, n], rr_sem.at[k, z], at_z(zz)
        )

    def lower(k):
        columns = pl.ds(pl.multiple_of(k * block, block), block)
        product = jnp.dot(lifted_v[...], down_v[:, columns], preferred_element_type=F32)
        okeep[k] = product[0:half]
        osend[k] = product[half : 2 * half].astype(BF16)
        pair_copy(k).start()

    def send_back(k):
        pair_copy(k).wait_recv()
        both = okeep[k] + orecv[k].astype(F32)
        rsend[k] = both.astype(BF16).reshape(nz, slots, block)
        for n in range(1, nz):
            back_copy(k, n).start()
        rrecv[k, z] = rsend[k, z]

    lower(0)

    def down_step(k):
        lower(k + 1)
        send_back(k)

    loop(chunks - 1, down_step)
    send_back(chunks - 1)

    def back_arrive(k):
        for n in range(1, nz):
            zz = z_next(n)
            remote(
                rsend.at[k, zz], rrecv.at[k, zz], rs_sem.at[k, 0], rr_sem.at[k, zz], partner
            ).wait_recv()
        total = rrecv[k, 0].astype(F32)
        for zz in range(1, nz):
            total = total + rrecv[k, zz].astype(F32)
        rrecv[k, 0] = total.astype(BF16)

    loop(chunks, back_arrive)
    summed = rrecv[:, 0].reshape(places, block)
    unorder = (
        lax.rem(lax.div(target, CAP), chunks) * slots
        + lax.div(target, pack) * CAP
        + lax.rem(target, CAP)
        == source
    ).astype(F32).astype(BF16)
    bsend[...] = (
        jnp.dot(unorder, summed, preferred_element_type=F32)
        .astype(BF16)
        .reshape(nexp, pack, block)
    )

    def return_copy(k):
        e = e_next(k)
        return remote(bsend.at[e], brecv.at[j], bs_sem.at[k], br_sem.at[j], at_e(e))

    loop(nexp - 1, lambda k: return_copy(k + 1).start())
    brecv[j] = bsend[j]

    def return_arrive(k):
        e = e_next(k + 1)
        remote(bsend.at[e], brecv.at[e], bs_sem.at[0], br_sem.at[e], partner).wait_recv()

    loop(nexp - 1, return_arrive)
    combined = jnp.dot(
        table_v[...], brecv[...].reshape(places, block), preferred_element_type=F32
    )
    result = (stream_v[...] + combined).astype(BF16)
    for k in range(chunks):
        out_ref[:, k * block : (k + 1) * block] = result[k * mine : (k + 1) * mine]

    for k in range(1, nctx):

        @pl.when(i + k < nctx)
        def _():
            state_copy(k).wait_send()

    swap.wait_send()
    for k in range(1, nz):
        mixed_copy(k).wait_send()
        zsum_copy(k).wait_send()

    def drain_exp(k):
        dispatch_copy(k + 1).wait_send()
        return_copy(k + 1).wait_send()
        loop(nz, lambda zz: psum_copy(zz, k + 1).wait_send())

    loop(nexp - 1, drain_exp)

    def drain_chunk(k):
        pair_copy(k).wait_send()
        for n in range(1, nz):
            rows_copy(k, n).wait_send()
            back_copy(k, n).wait_send()
        for zz in range(nz):
            forward_copy(k, zz).wait_send()

    loop(chunks, drain_chunk)


def shards(nctx, nexp, *arrays):
    (
        mixer_input,
        mixer_gate,
        step_size,
        write_coeffs,
        read_coeffs,
        decay_rates,
        skip_scale,
        out_weight,
        residual_in,
        norm_gain,
        expert_ids,
        gate_weights,
        up_weight,
        down_weight,
    ) = arrays
    tokens, channels = mixer_input.shape
    states = write_coeffs.shape[1]
    mine, width = residual_in.shape
    hidden = up_weight.shape[2]
    nz = nctx // 2
    block = width // nctx
    chunks = nctx
    slots = nexp * CAP
    pack = chunks * CAP
    operands = (
        mixer_input,
        mixer_gate,
        step_size,
        write_coeffs.T,
        read_coeffs.T,
        decay_rates.T,
        skip_scale.reshape(1, channels),
        out_weight,
        residual_in,
        norm_gain.reshape(1, width),
        expert_ids.T,
        gate_weights.T,
        up_weight.reshape(width, hidden),
        down_weight.reshape(hidden, width),
    )
    dma = pltpu.SemaphoreType.DMA
    scratch = [
        pltpu.VMEM((tokens, channels), BF16),
        pltpu.VMEM((tokens, channels), BF16),
        pltpu.VMEM((tokens, channels), BF16),
        pltpu.VMEM((states, tokens), F32),
        pltpu.VMEM((states, tokens), F32),
        pltpu.VMEM((states, channels), F32),
        pltpu.VMEM((1, channels), F32),
        pltpu.VMEM((mine, width), BF16),
        pltpu.VMEM((1, width), F32),
        pltpu.VMEM((2, mine), jnp.int32),
        pltpu.VMEM((2, mine), BF16),
        pltpu.VMEM((tokens, states), F32),
        pltpu.VMEM((tokens, states), F32),
        pltpu.VMEM((width, hidden), BF16),
        pltpu.VMEM((hidden, width), BF16),
        pltpu.VMEM((2, channels, block), BF16),
        pltpu.VMEM((tokens, channels), F32),
        pltpu.VMEM((tokens, channels), F32),
        pltpu.VMEM((tokens, states, 128), F32),
        pltpu.VMEM((tokens, states, 128), F32),
        pltpu.VMEM((states, channels), F32),
        pltpu.VMEM((states, channels), F32),
        pltpu.VMEM((states + 8, channels), F32),
        pltpu.VMEM((nctx, states + 8, channels), F32),
        pltpu.VMEM((nz, tokens, channels), BF16),
        pltpu.VMEM((nexp, nz * 2 * mine, block), BF16),
        pltpu.VMEM((nexp, nz * 2 * mine, block), BF16),
        pltpu.VMEM((nz, 2 * mine, block), F32),
        pltpu.VMEM((nz, 2 * mine, block), F32),
        pltpu.VMEM((chunks * mine, block), F32),
        pltpu.VMEM((chunks * mine, nexp * pack), BF16),
        pltpu.VMEM((nexp, pack, block), BF16),
        pltpu.VMEM((nexp, pack, block), BF16),
        pltpu.VMEM((chunks, nctx * slots, block), BF16),
        pltpu.VMEM((nctx * slots, hidden), F32),
        pltpu.VMEM((nctx * slots, hidden), BF16),
        pltpu.VMEM((chunks, nz * slots, block), BF16),
        pltpu.VMEM((chunks, nz * slots, block), BF16),
        pltpu.VMEM((chunks, nz * slots, block), F32),
        pltpu.VMEM((chunks, nz, slots, block), BF16),
        pltpu.VMEM((chunks, nz, slots, block), BF16),
        pltpu.VMEM((nexp, pack, block), BF16),
        pltpu.VMEM((nexp, pack, block), BF16),
        dma((12,)),
        dma((2, chunks)),
        dma((2,)),
        dma((nctx,)),
        dma((nctx,)),
        dma((nz,)),
        dma((nz,)),
        dma((nz, nexp)),
        dma((nz, nexp)),
        dma((nz,)),
        dma((nz,)),
        dma((nexp,)),
        dma((nexp,)),
        dma((chunks, nz)),
        dma((chunks, nz)),
        dma((chunks, nz)),
        dma((chunks, nz)),
        dma((chunks,)),
        dma((chunks,)),
        dma((chunks, nz)),
        dma((chunks, nz)),
        dma((nexp,)),
        dma((nexp,)),
    ]
    return pl.pallas_call(
        functools.partial(kernel, nctx, nexp),
        out_shape=jax.ShapeDtypeStruct((mine, width), BF16),
        in_specs=[pl.BlockSpec(memory_space=pl.ANY)] * len(operands),
        out_specs=pl.BlockSpec(memory_space=pltpu.VMEM),
        scratch_shapes=scratch,
        compiler_params=pltpu.CompilerParams(
            collective_id=0, has_side_effects=True, vmem_limit_bytes=60 * 2**20
        ),
    )(*operands)


def solution(mesh):
    return jax.shard_map(
        functools.partial(shards, mesh.shape["ctx"], mesh.shape["exp"]),
        mesh=mesh,
        in_specs=(
            P("ctx", "exp"),
            P("ctx", "exp"),
            P("ctx", "exp"),
            P("ctx", None),
            P("ctx", None),
            P("exp", None),
            P("exp"),
            P("exp", "ctx"),
            P(("ctx", "exp"), None),
            P(),
            P(("ctx", "exp"), None),
            P(("ctx", "exp"), None),
            P("exp", None, "ctx"),
            P("exp", "ctx", None),
        ),
        out_specs=P(("ctx", "exp"), None),
        check_vma=False,
    )
```

```python
import functools
import math

import jax
import jax.numpy as jnp
from jax import lax
from jax.experimental import pallas as pl
from jax.experimental.pallas import tpu as pltpu
from jax.sharding import PartitionSpec as P

MESH = pl.DeviceIdType.MESH
CAP = 2
EPSILON = 1e-05
LOG2E = math.log2(math.e)
F32 = jnp.float32
BF16 = jnp.bfloat16
STEPS = 16


def remote(src, dst, send_sem, recv_sem, device):
    return pltpu.make_async_remote_copy(
        src_ref=src,
        dst_ref=dst,
        send_sem=send_sem,
        recv_sem=recv_sem,
        device_id=device,
        device_id_type=MESH,
    )


def loop(count, body):
    def step(k, carry):
        body(k)
        return carry

    lax.fori_loop(0, count, step, 0)


def kernel(
    nctx,
    nexp,
    x_hbm,
    gate_hbm,
    step_hbm,
    write_hbm,
    read_hbm,
    rates_hbm,
    skip_hbm,
    ow_hbm,
    res_hbm,
    gain_hbm,
    ids_hbm,
    pairgate_hbm,
    up_hbm,
    down_hbm,
    out_ref,
    x_v,
    gate_v,
    step_v,
    write_v,
    read_v,
    rates_v,
    skip_v,
    res_v,
    gain_v,
    ids_v,
    pairgate_v,
    write_t,
    read_t,
    up_v,
    down_v,
    w_v,
    dt_f,
    u_f,
    wb_v,
    rb_v,
    rate2_v,
    h_v,
    hsend,
    hrecv,
    tsend,
    trecv,
    meta_v,
    metas,
    mixed_v,
    near_send,
    near_recv,
    far_send,
    far_recv,
    stream_v,
    table_v,
    gated_v,
    order_v,
    nrows,
    lsend,
    lrecv,
    qsend,
    qrecv,
    rows_v,
    acc_v,
    lifted_v,
    osend,
    orecv,
    okeep,
    rsum,
    lsum,
    rsend,
    rrecv,
    qsend2,
    qrecv2,
    lsend2,
    lrecv2,
    csend,
    crecv,
    lsem,
    wsem,
    wswap,
    hs_sem,
    hr_sem,
    ms_sem,
    mr_sem,
    ps_sem,
    pr_sem,
    zs_sem,
    zr_sem,
    mt_sem,
    ns_sem,
    nr_sem,
    ls_sem,
    lr_sem,
    qs_sem,
    qr_sem,
    xs_sem,
    xr_sem,
    fs_sem,
    fr_sem,
    gs_sem,
    gr_sem,
    os_sem,
    or_sem,
    rs_sem,
    rr_sem,
    hq_sem,
    hl_sem,
    cs_sem,
):
    i = lax.axis_index("ctx")
    j = lax.axis_index("exp")
    nz = nctx // 2
    z = lax.div(i, 2)
    c = lax.rem(i, 2)
    nx = math.isqrt(nexp)
    y, x = lax.div(j, nx), lax.rem(j, nx)
    partner = (z * 2 + 1 - c, j)
    tokens, channels = x_hbm.shape
    states = write_hbm.shape[0]
    mine, width = res_hbm.shape
    block = width // nctx
    hidden = up_hbm.shape[1]
    chunks = nctx
    parts = 2 * chunks
    slots = nexp * CAP
    half = nz * slots

    def at_z(zz):
        return (zz * 2 + c, j)

    def at_e(e):
        return (i, e)

    def z_next(k):
        return lax.rem(z + k, nz)

    def e_next(k):
        return lax.rem(j + k, nexp)

    small = [
        (write_hbm, write_v),
        (read_hbm, read_v),
        (rates_hbm, rates_v),
        (step_hbm, step_v),
        (x_hbm, x_v),
        (gate_hbm, gate_v),
        (skip_hbm, skip_v),
        (res_hbm, res_v),
        (gain_hbm, gain_v),
        (ids_hbm, ids_v),
        (pairgate_hbm, pairgate_v),
        (ow_hbm, w_v.at[c]),
    ]
    small = [
        pltpu.make_async_copy(src, dst, lsem.at[n]) for n, (src, dst) in enumerate(small)
    ]
    for copy in small:
        copy.start()

    barrier = pltpu.get_barrier_semaphore()

    def greet_ctx(k):
        pl.semaphore_signal(
            barrier, inc=1, device_id=(lax.rem(i + k + 1, nctx), j), device_id_type=MESH
        )

    loop(nctx - 1, greet_ctx)
    for k in range(1, nx):
        for e in (y * nx + lax.rem(x + k, nx), lax.rem(y + k, nx) * nx + x):
            pl.semaphore_signal(barrier, inc=1, device_id=at_e(e), device_id_type=MESH)

    def up_copy(k):
        part = pl.ds(pl.multiple_of(k * block, block), block)
        return pltpu.make_async_copy(up_hbm.at[part], up_v.at[part], wsem.at[0, k])

    depth = hidden // chunks

    def down_copy(k):
        part = pl.ds(pl.multiple_of(k * depth, depth), depth)
        return pltpu.make_async_copy(down_hbm.at[part], down_v.at[part], wsem.at[1, k])

    loop(chunks, lambda k: up_copy(k).start())
    loop(chunks, lambda k: down_copy(k).start())

    small[0].wait()
    small[1].wait()
    write_t[...] = write_v[...].T
    read_t[...] = read_v[...].T
    diagonal = lax.broadcasted_iota(jnp.int32, (1, states, states), 1) == lax.broadcasted_iota(
        jnp.int32, (1, states, states), 2
    )

    def spread(n):
        part = pl.ds(pl.multiple_of(n * STEPS, STEPS), STEPS)
        for source, wide in ((write_t, wb_v), (read_t, rb_v)):
            rows = jnp.broadcast_to(source[part, :][:, None, :], (STEPS, states, states))
            picked = jnp.sum(jnp.where(diagonal, rows, 0.0), axis=2, keepdims=True)
            wide[part] = jnp.broadcast_to(picked, (STEPS, states, 128))

    loop(tokens // STEPS, spread)
    small[2].wait()
    rate2_v[...] = rates_v[...] * (-LOG2E)
    small[3].wait()
    small[4].wait()

    def widen(n):
        part = pl.ds(pl.multiple_of(n * STEPS, STEPS), STEPS)
        steps = step_v[part, :].astype(F32)
        dt_f[part, :] = steps
        u_f[part, :] = steps * x_v[part, :].astype(F32)

    loop(tokens // STEPS, widen)
    copies = channels // 128

    def advance(h, t, rate2):
        decay = jnp.exp2(dt_f[pl.ds(t, 1), :] * rate2)
        push = u_f[pl.ds(t, 1), :] * jnp.concatenate([wb_v[t]] * copies, axis=1)
        return decay * h + push

    def first(n, carry):
        h, total = carry
        rate2 = rate2_v[...]
        for r in range(STEPS):
            h = advance(h, n * STEPS + r, rate2)
        part = pl.ds(pl.multiple_of(n * STEPS, STEPS), STEPS)
        return h, total + jnp.sum(dt_f[part, :], axis=0, keepdims=True)

    h, total = lax.fori_loop(
        0,
        tokens // STEPS,
        first,
        (jnp.zeros((states, channels), F32), jnp.zeros((1, channels), F32)),
    )
    hsend[...] = h.astype(BF16)
    folded = jnp.concatenate([total[:, q * 128 : (q + 1) * 128] for q in range(copies)], axis=0)
    tsend[...] = jnp.concatenate([folded] * (8 // copies), axis=0)
    meta_v[...] = jnp.zeros_like(meta_v)
    small[9].wait()
    small[10].wait()
    meta_v[0:2, 0:mine] = ids_v[...].astype(F32)
    meta_v[2:4, 0:mine] = pairgate_v[...].astype(F32)

    pl.semaphore_wait(barrier, nctx - 1 + 2 * (nx - 1))

    def state_copies(k):
        device = (lax.rem(i + k, nctx), j)
        return (
            remote(tsend, trecv.at[i], hs_sem.at[0, k], hr_sem.at[0, i], device),
            remote(hsend, hrecv.at[i], hs_sem.at[1, k], hr_sem.at[1, i], device),
        )

    for k in range(1, nctx):

        @pl.when(i + k < nctx)
        def _():
            for copy in state_copies(k):
                copy.start()

    def drain_states():
        for k in range(1, nctx):

            @pl.when(i + k < nctx)
            def _():
                for copy in state_copies(k):
                    copy.wait_send()

    sent = [drain_states]

    def meta_copy(k):
        return remote(
            meta_v, metas.at[z], mt_sem.at[0, k], mt_sem.at[1, z], at_z(z_next(k))
        )

    small[11].wait()
    swap = remote(w_v.at[c], w_v.at[c], wswap.at[0], wswap.at[1], partner)
    swap.start()
    sent.append(swap.wait_send)

    h_v[...] = jnp.zeros_like(h_v)
    for k in range(nctx - 1):

        @pl.when(k < i)
        def _():
            remote(tsend, trecv.at[k], hs_sem.at[0, 0], hr_sem.at[0, k], partner).wait_recv()
            remote(hsend, hrecv.at[k], hs_sem.at[1, 0], hr_sem.at[1, k], partner).wait_recv()
            passed = jnp.concatenate([trecv[k, q : q + 1, :] for q in range(copies)], axis=1)
            h_v[...] = jnp.exp2(rate2_v[...] * passed) * h_v[...] + hrecv[k].astype(F32)

    for k in range(1, nz):
        meta_copy(k).start()
    metas[z] = meta_v[...]
    sent.append(lambda: [meta_copy(k).wait_send() for k in range(1, nz)])

    small[5].wait()
    small[6].wait()

    def second(n, h):
        part = pl.ds(pl.multiple_of(n * STEPS, STEPS), STEPS)
        rate2 = rate2_v[...]
        reads = []
        for r in range(STEPS):
            t = n * STEPS + r
            h = advance(h, t, rate2)
            seen = h * jnp.concatenate([rb_v[t]] * copies, axis=1)
            reads.append(jnp.sum(seen, axis=0, keepdims=True))
        readout = jnp.concatenate(reads, axis=0)
        readout = readout + skip_v[...] * x_v[part, :].astype(F32)
        gate = gate_v[part, :].astype(F32)
        mixed_v[z, part, :] = (readout * (gate / (1.0 + jnp.exp(-gate)))).astype(BF16)
        return h

    lax.fori_loop(0, tokens // STEPS, second, h_v[...])

    def mixed_copy(k):
        return remote(
            mixed_v.at[z], mixed_v.at[z], ms_sem.at[k], mr_sem.at[z], at_z(z_next(k))
        )

    for k in range(1, nz):
        mixed_copy(k).start()
    sent.append(lambda: [mixed_copy(k).wait_send() for k in range(1, nz)])

    swap.wait_recv()

    def line(side, n):
        return at_e(y * nx + n) if side == 0 else at_e(n * nx + x)

    def line_of(side):
        return x if side == 0 else y

    def line_next(side, k):
        return lax.rem(line_of(side) + k, nx)

    def near_copy(side, zz, k):
        n = line_next(side, k)
        return remote(
            near_send.at[side, zz, n],
            near_recv.at[side, zz, line_of(side)],
            ps_sem.at[side, zz, k],
            pr_sem.at[side, zz, line_of(side)],
            line(side, n),
        )

    def farthest_last(k):
        return k + lax.div(k, 2) * (5 - 2 * k) if nz == 4 else k

    def project(k):
        zz = z_next(farthest_last(k))

        @pl.when(k > 0)
        def _():
            remote(
                mixed_v.at[zz], mixed_v.at[zz], ms_sem.at[0], mr_sem.at[zz], partner
            ).wait_recv()

        for side in range(2):
            part = jnp.dot(mixed_v[zz], w_v[side], preferred_element_type=F32)
            part = part.reshape(nx, nx, mine, block)
            if side == 0:
                part = jnp.stack(
                    [
                        jnp.concatenate([part[b, a] for b in range(nx)], axis=0)
                        for a in range(nx)
                    ]
                )
            near_send[side, zz] = part.reshape(nx, nx * mine, block).astype(BF16)
            for n in range(1, nx):
                near_copy(side, zz, n).start()
            near_recv[side, zz, line_of(side)] = near_send[side, zz, line_of(side)]

    sent.append(
        lambda: loop(
            nz,
            lambda zz: [
                near_copy(side, zz, n).wait_send() for side in range(2) for n in range(1, nx)
            ],
        )
    )

    def far_line(side, zz, n):
        if side == 0:
            return (zz * 2 + c, n * nx + x)
        return (zz * 2 + c, y * nx + n)

    def far_copy(side, zz, k):
        n = line_next(1 - side, k)
        return remote(
            far_send.at[side, zz, n],
            far_recv.at[side, z, line_of(1 - side)],
            zs_sem.at[side, zz, k],
            zr_sem.at[side, z, line_of(1 - side)],
            far_line(side, zz, n),
        )

    def far_out(k):
        zz = z_next(farthest_last(k))
        for side in range(2):
            for n in range(1, nx):
                m = line_next(side, n)
                remote(
                    near_send.at[side, zz, m],
                    near_recv.at[side, zz, m],
                    ps_sem.at[side, zz, 0],
                    pr_sem.at[side, zz, m],
                    partner,
                ).wait_recv()
            part = near_recv[side, zz, 0].astype(F32)
            for n in range(1, nx):
                part = part + near_recv[side, zz, n].astype(F32)
            part = part.reshape(nx, mine, block)
            part = jnp.concatenate([part[:, :, : block // 2], part[:, :, block // 2 :]], axis=1)
            far_send[side, zz] = part.astype(BF16)

            @pl.when(k == 0)
            def _():
                me = line_of(1 - side)
                far_recv[side, zz, me] = far_send[side, zz, me]

            @pl.when(k > 0)
            def _():
                far_copy(side, zz, 0).start()

            for n in range(1, nx):
                far_copy(side, zz, n).start()

    project(0)
    far_out(0)
    loop(nz - 1, lambda k: project(k + 1))
    loop(nz - 1, lambda k: far_out(k + 1))

    def drain_far():
        for side in range(2):
            for k in range(nz):
                for n in range(0 if k else 1, nx):
                    far_copy(side, z_next(k), n).wait_send()

    sent.append(drain_far)

    small[7].wait()
    small[8].wait()
    wide = width // parts
    hold = parts // 2
    pack = hold * CAP
    stacked = hold * mine
    places = nexp * pack
    lanes = lax.broadcasted_iota(jnp.int32, (mine, 128), 1)
    square = lax.broadcasted_iota(jnp.int32, (mine, mine), 0) == lax.broadcasted_iota(
        jnp.int32, (mine, mine), 1
    )
    earlier = (
        lax.broadcasted_iota(jnp.int32, (mine, mine), 0)
        > lax.broadcasted_iota(jnp.int32, (mine, mine), 1)
    ).astype(F32)
    column = lax.broadcasted_iota(jnp.int32, (stacked, places), 1)
    row = lax.broadcasted_iota(jnp.int32, (stacked, places), 0)
    column_slot = lax.div(column, pack) * CAP + lax.rem(column, CAP)
    same_part = lax.rem(lax.div(column, CAP), hold) == lax.div(row, mine)

    def column_of(values):
        return jnp.sum(jnp.where(square, values, 0.0), axis=1, keepdims=True)

    def tables(zz):
        meta = metas[zz]
        idents = [column_of(meta[n : n + 1, 0:mine]).astype(jnp.int32) for n in range(2)]
        hots = [(lanes == ident).astype(F32) for ident in idents]
        before = jnp.dot(earlier, hots[0] + hots[1], preferred_element_type=F32)
        table = jnp.zeros((stacked, places), F32)
        gated = jnp.zeros((stacked, places), F32)
        for n in range(2):
            rank = jnp.sum(before * hots[n], axis=1, keepdims=True).astype(jnp.int32)
            slot = jnp.concatenate([idents[n] * CAP + rank] * hold, axis=0)
            taken = jnp.where(same_part & (column_slot == slot), 1.0, 0.0)
            weight = column_of(meta[n + 2 : n + 3, 0:mine])
            table = table + taken
            gated = gated + taken * jnp.concatenate([weight] * hold, axis=0)
        gated_v[zz] = gated.astype(BF16)
        table_v[zz] = table.T.astype(BF16)

    tables(z)

    def other_tables(k):
        zz = z_next(k + 1)
        remote(meta_v, metas.at[zz], mt_sem.at[0, 0], mt_sem.at[1, zz], partner).wait_recv()
        tables(zz)

    loop(nz - 1, other_tables)

    source = lax.broadcasted_iota(jnp.int32, (places, places), 1)
    target = lax.broadcasted_iota(jnp.int32, (places, places), 0)

    def by_part(index):
        return (
            lax.rem(lax.div(index, CAP), hold) * slots
            + lax.div(index, pack) * CAP
            + lax.rem(index, CAP)
        )

    order_v[0] = (by_part(source) == target).astype(F32).astype(BF16)
    order_v[1] = (by_part(target) == source).astype(F32).astype(BF16)

    def stack(wide_rows):
        return jnp.concatenate(
            [wide_rows[:, k * wide : (k + 1) * wide] for k in range(parts)], axis=0
        )

    res = stack(res_v[...].astype(F32))
    gain = stack(jnp.broadcast_to(gain_v[...], (mine, width)))
    for side in range(2):
        for k in range(nz):
            for n in range(0 if k else 1, nx):
                zz, m = z_next(k), line_next(1 - side, n)
                remote(
                    far_send.at[side, zz, m],
                    far_recv.at[side, zz, m],
                    zs_sem.at[side, zz, 0],
                    zr_sem.at[side, zz, m],
                    partner,
                ).wait_recv()
    summed_parts = []
    for zz in range(nz):
        for side in range(2):
            part = far_recv[side, zz, 0].astype(F32)
            for n in range(1, nx):
                part = part + far_recv[side, zz, n].astype(F32)
            summed_parts.append(part)
    stream = (res + jnp.concatenate(summed_parts, axis=0)).astype(BF16).astype(F32)
    stream_v[...] = stream
    squares = jnp.sum(stream * stream, axis=1, keepdims=True).reshape(parts, mine, 1)
    scale = lax.rsqrt(jnp.sum(squares, axis=0) / width + EPSILON)
    normed = (stream * jnp.concatenate([scale] * parts, axis=0) * gain).astype(BF16)

    nrows[z] = normed[stacked:]

    def norm_copy(k):
        return remote(nrows.at[z], nrows.at[z], ns_sem.at[k], nr_sem.at[z], at_z(z_next(k)))

    for k in range(1, nz):
        norm_copy(k).start()
    sent.append(lambda: [norm_copy(k).wait_send() for k in range(1, nz)])

    def slotted(zz, rows):
        return (
            jnp.dot(table_v[zz], rows, preferred_element_type=F32)
            .astype(BF16)
            .reshape(nexp, pack, wide)
        )

    def left_copy(k):
        e = e_next(k)
        return remote(lsend.at[e], lrecv.at[j], ls_sem.at[k], lr_sem.at[j], at_e(e))

    lsend[...] = slotted(z, normed[:stacked])
    loop(nexp - 1, lambda k: left_copy(k + 1).start())
    lrecv[j] = lsend[j]
    sent.append(lambda: loop(nexp - 1, lambda k: left_copy(k + 1).wait_send()))

    def right_copy(k, first):
        e = e_next(k)
        which = pl.ds(0, 1) if first else pl.ds(1, nz - 1)
        n = 0 if first else 1
        return remote(
            qsend.at[e, which],
            qrecv.at[j, which],
            qs_sem.at[n, k],
            qr_sem.at[n, j],
            at_e(e),
        )

    qsend[:, 0] = slotted(z, normed[stacked:])
    loop(nexp - 1, lambda k: right_copy(k + 1, True).start())

    def right_slots(k):
        zz = z_next(k + 1)
        remote(nrows.at[zz], nrows.at[zz], ns_sem.at[0], nr_sem.at[zz], partner).wait_recv()
        qsend[:, k + 1] = slotted(zz, nrows[zz])

    loop(nz - 1, right_slots)
    loop(nexp - 1, lambda k: right_copy(k + 1, False).start())
    qrecv[j] = qsend[j]
    sent.append(
        lambda: loop(
            nexp - 1,
            lambda k: [right_copy(k + 1, first).wait_send() for first in (True, False)],
        )
    )

    def left_arrive(k):
        e = e_next(k + 1)
        remote(lsend.at[e], lrecv.at[e], ls_sem.at[0], lr_sem.at[e], partner).wait_recv()

    def rows_part(zz):
        return pl.ds(pl.multiple_of(zz * slots, slots), slots)

    def arranged(rows):
        return (
            jnp.dot(order_v[0], rows.reshape(places, wide), preferred_element_type=F32)
            .astype(BF16)
            .reshape(hold, slots, wide)
        )

    def rows_copy(g, n):
        here = rows_v.at[pl.ds(g * group, group), rows_part(z)]
        return remote(here, here, xs_sem.at[g, n], xr_sem.at[g, z], at_z(z_next(n)))

    def forward_copy(g, zz):
        return remote(
            rows_v.at[pl.ds(g * group, group), rows_part(zz)],
            rows_v.at[pl.ds(g * group, group), pl.ds(pl.multiple_of(half + zz * slots, slots), slots)],
            fs_sem.at[g, zz],
            fr_sem.at[g, zz],
            partner,
        )

    def right_forward(g):
        at = pl.ds(hold + g * group, group)
        return remote(
            rows_v.at[at, pl.ds(0, half)],
            rows_v.at[at, pl.ds(half, half)],
            gs_sem.at[g],
            gr_sem.at[g],
            partner,
        )

    group = hold // 2
    loop(nexp - 1, left_arrive)
    rows_v[0:hold, rows_part(z), :] = arranged(lrecv[...])
    for g in range(2):
        for n in range(1, nz):
            rows_copy(g, n).start()
        forward_copy(g, z).start()

    def right_arrive(n):
        which = pl.ds(0, 1) if n == 0 else pl.ds(1, nz - 1)

        def one(k):
            e = e_next(k + 1)
            remote(
                qsend.at[e, which], qrecv.at[e, which], qs_sem.at[n, 0], qr_sem.at[n, e], partner
            ).wait_recv()

        loop(nexp - 1, one)

    def right_rows(k):
        rows_v[hold:parts, rows_part(z_next(k)), :] = arranged(qrecv[:, k])

    right_arrive(0)
    right_rows(0)
    for g in range(2):
        for n in range(1, nz):
            zz = z_next(farthest_last(n))
            there = rows_v.at[pl.ds(g * group, group), rows_part(zz)]
            remote(there, there, xs_sem.at[g, 0], xr_sem.at[g, zz], partner).wait_recv()
            forward_copy(g, zz).start()
    right_arrive(1)
    loop(nz - 1, lambda k: right_rows(k + 1))
    for g in range(2):
        right_forward(g).start()

    def drain_rows():
        for g in range(2):
            right_forward(g).wait_send()
            for n in range(1, nz):
                rows_copy(g, n).wait_send()
            for zz in range(nz):
                forward_copy(g, zz).wait_send()

    sent.append(drain_rows)

    tile = 512 if hidden % 512 == 0 else hidden
    tiles = hidden // tile

    def tile_columns(n):
        return pl.ds(pl.multiple_of(n * tile, tile), tile)

    def half_product(first, columns):
        start = 0 if first else hold
        rows = jnp.concatenate([rows_v[start + k] for k in range(hold)], axis=1)
        weights = up_v[start * wide : (start + hold) * wide, columns]
        return jnp.dot(rows, weights, preferred_element_type=F32)

    loop(chunks, lambda k: up_copy(k).wait())
    for g in range(2):
        for zz in range(nz):
            forward_copy(g, zz).wait_recv()

    def lift_left(n):
        columns = tile_columns(n)
        acc_v[:, columns] = half_product(True, columns)

    loop(tiles, lift_left)
    for g in range(2):
        right_forward(g).wait_recv()

    def lift_right(n):
        columns = tile_columns(n)
        lifted = acc_v[:, columns] + half_product(False, columns)
        lifted_v[:, columns] = (lifted / (1.0 + jnp.exp(-lifted))).astype(BF16)

    loop(tiles, lift_right)
    loop(chunks, lambda k: down_copy(k).wait())

    halves = chunks // 2

    def step_of(k):
        return lax.rem(k + halves, chunks)

    def pair_copy(k):
        return remote(osend.at[k], orecv.at[k], os_sem.at[k], or_sem.at[k], partner)

    def lower(n):
        k = step_of(n)
        columns = pl.ds(pl.multiple_of(k * block, block), block)
        product = jnp.dot(lifted_v[...], down_v[:, columns], preferred_element_type=F32)
        okeep[k] = product[0:half]
        osend[k] = product[half : 2 * half].astype(BF16)
        pair_copy(k).start()

    def paired(k):
        pair_copy(k).wait_recv()
        return okeep[k] + orecv[k].astype(F32)

    def keep_right(n):
        both = paired(halves + n).astype(BF16)
        for q in range(2):
            rsum[2 * n + q] = both[:, q * wide : (q + 1) * wide].reshape(nz, slots, wide)

    lower(0)

    def right_step(n):
        lower(n + 1)
        keep_right(n)

    loop(halves, right_step)

    def unarranged(rows):
        return (
            jnp.dot(order_v[1], rows.reshape(places, wide), preferred_element_type=F32)
            .astype(BF16)
            .reshape(nexp, pack, wide)
        )

    def home_right_copy(k):
        e = e_next(k)
        return remote(qsend2.at[e], qrecv2.at[j], hq_sem.at[0, k], hq_sem.at[1, j], at_e(e))

    def home_right(k):
        qsend2[:, k] = unarranged(rsum[:, z_next(k)])

    loop(nz, home_right)
    loop(nexp - 1, lambda k: home_right_copy(k + 1).start())
    qrecv2[j] = qsend2[j]
    sent.append(lambda: loop(nexp - 1, lambda k: home_right_copy(k + 1).wait_send()))

    def back_copy(k, n):
        zz = z_next(n)
        return remote(
            rsend.at[k, zz], rrecv.at[k, z], rs_sem.at[k, n], rr_sem.at[k, z], at_z(zz)
        )

    def send_back(k):
        rsend[k] = paired(k).astype(BF16).reshape(nz, slots, block)
        for n in range(1, nz):
            back_copy(k, n).start()
        rrecv[k, z] = rsend[k, z]

    def left_step(n):
        lower(n + halves + 1)
        send_back(n)

    loop(halves - 1, left_step)
    send_back(halves - 1)

    def drain_back(k):
        for n in range(1, nz):
            back_copy(k, n).wait_send()

    sent.append(lambda: loop(halves, drain_back))
    sent.append(lambda: loop(chunks, lambda k: pair_copy(k).wait_send()))

    def back_arrive(k):
        for n in range(1, nz):
            zz = z_next(n)
            remote(
                rsend.at[k, zz], rrecv.at[k, zz], rs_sem.at[k, 0], rr_sem.at[k, zz], partner
            ).wait_recv()
        total = rrecv[k, 0].astype(F32)
        for zz in range(1, nz):
            total = total + rrecv[k, zz].astype(F32)
        for q in range(2):
            lsum[2 * k + q] = total[:, q * wide : (q + 1) * wide].astype(BF16)

    loop(halves, back_arrive)
    lsend2[...] = unarranged(lsum[...])

    def home_left_copy(k):
        e = e_next(k)
        return remote(lsend2.at[e], lrecv2.at[j], hl_sem.at[0, k], hl_sem.at[1, j], at_e(e))

    loop(nexp - 1, lambda k: home_left_copy(k + 1).start())
    lrecv2[j] = lsend2[j]
    sent.append(lambda: loop(nexp - 1, lambda k: home_left_copy(k + 1).wait_send()))

    def home_right_arrive(k):
        e = e_next(k + 1)
        remote(
            qsend2.at[e], qrecv2.at[e], hq_sem.at[0, 0], hq_sem.at[1, e], partner
        ).wait_recv()

    loop(nexp - 1, home_right_arrive)

    def weighed(zz, rows):
        return jnp.dot(gated_v[zz], rows.reshape(places, wide), preferred_element_type=F32)

    def token_copy(k):
        zz = z_next(k)
        return remote(csend.at[zz], crecv.at[z], cs_sem.at[0, k], cs_sem.at[1, z], at_z(zz))

    for n in range(1, nz):
        k = n + n // 2 * (5 - 2 * n) if nz == 4 else n
        zz = z_next(k)
        csend[zz] = weighed(zz, qrecv2[:, k]).astype(BF16)
        token_copy(k).start()
    crecv[z] = weighed(z, qrecv2[:, 0]).astype(BF16)
    sent.append(lambda: [token_copy(k).wait_send() for k in range(1, nz)])

    def home_left_arrive(k):
        e = e_next(k + 1)
        remote(
            lsend2.at[e], lrecv2.at[e], hl_sem.at[0, 0], hl_sem.at[1, e], partner
        ).wait_recv()

    def give(first, rows):
        for k in range(hold):
            at = (0 if first else hold) + k
            out_ref[:, at * wide : (at + 1) * wide] = rows[k * mine : (k + 1) * mine].astype(BF16)

    loop(nexp - 1, home_left_arrive)
    give(True, stream_v[0:stacked] + weighed(z, lrecv2[...]))
    for k in range(1, nz):
        zz = z_next(k)
        remote(
            csend.at[zz], crecv.at[zz], cs_sem.at[0, 0], cs_sem.at[1, zz], partner
        ).wait_recv()
    total = stream_v[stacked : 2 * stacked]
    for zz in range(nz):
        total = total + crecv[zz].astype(F32)
    give(False, total)

    for drain in sent:
        drain()


def shards(nctx, nexp, *arrays):
    (
        mixer_input,
        mixer_gate,
        step_size,
        write_coeffs,
        read_coeffs,
        decay_rates,
        skip_scale,
        out_weight,
        residual_in,
        norm_gain,
        expert_ids,
        gate_weights,
        up_weight,
        down_weight,
    ) = arrays
    tokens, channels = mixer_input.shape
    states = write_coeffs.shape[1]
    mine, width = residual_in.shape
    hidden = up_weight.shape[2]
    nz = nctx // 2
    nx = math.isqrt(nexp)
    block = width // nctx
    chunks = nctx
    slots = nexp * CAP
    parts = 2 * chunks
    wide = width // parts
    hold = parts // 2
    pack = hold * CAP
    stacked = hold * mine
    places = nexp * pack
    operands = (
        mixer_input,
        mixer_gate,
        step_size,
        write_coeffs.T,
        read_coeffs.T,
        decay_rates.T,
        skip_scale.reshape(1, channels),
        out_weight,
        residual_in,
        norm_gain.reshape(1, width),
        expert_ids.T,
        gate_weights.T,
        up_weight.reshape(width, hidden),
        down_weight.reshape(hidden, width),
    )
    dma = pltpu.SemaphoreType.DMA
    scratch = [
        pltpu.VMEM((tokens, channels), BF16),
        pltpu.VMEM((tokens, channels), BF16),
        pltpu.VMEM((tokens, channels), BF16),
        pltpu.VMEM((states, tokens), F32),
        pltpu.VMEM((states, tokens), F32),
        pltpu.VMEM((states, channels), F32),
        pltpu.VMEM((1, channels), F32),
        pltpu.VMEM((mine, width), BF16),
        pltpu.VMEM((1, width), F32),
        pltpu.VMEM((2, mine), jnp.int32),
        pltpu.VMEM((2, mine), BF16),
        pltpu.VMEM((tokens, states), F32),
        pltpu.VMEM((tokens, states), F32),
        pltpu.VMEM((width, hidden), BF16),
        pltpu.VMEM((hidden, width), BF16),
        pltpu.VMEM((2, channels, block), BF16),
        pltpu.VMEM((tokens, channels), F32),
        pltpu.VMEM((tokens, channels), F32),
        pltpu.VMEM((tokens, states, 128), F32),
        pltpu.VMEM((tokens, states, 128), F32),
        pltpu.VMEM((states, channels), F32),
        pltpu.VMEM((states, channels), F32),
        pltpu.VMEM((states, channels), BF16),
        pltpu.VMEM((nctx, states, channels), BF16),
        pltpu.VMEM((8, 128), F32),
        pltpu.VMEM((nctx, 8, 128), F32),
        pltpu.VMEM((8, 128), F32),
        pltpu.VMEM((nz, 8, 128), F32),
        pltpu.VMEM((nz, tokens, channels), BF16),
        pltpu.VMEM((2, nz, nx, nx * mine, block), BF16),
        pltpu.VMEM((2, nz, nx, nx * mine, block), BF16),
        pltpu.VMEM((2, nz, nx, 2 * mine, wide), BF16),
        pltpu.VMEM((2, nz, nx, 2 * mine, wide), BF16),
        pltpu.VMEM((parts * mine, wide), F32),
        pltpu.VMEM((nz, places, stacked), BF16),
        pltpu.VMEM((nz, stacked, places), BF16),
        pltpu.VMEM((2, places, places), BF16),
        pltpu.VMEM((nz, stacked, wide), BF16),
        pltpu.VMEM((nexp, pack, wide), BF16),
        pltpu.VMEM((nexp, pack, wide), BF16),
        pltpu.VMEM((nexp, nz, pack, wide), BF16),
        pltpu.VMEM((nexp, nz, pack, wide), BF16),
        pltpu.VMEM((parts, nctx * slots, wide), BF16),
        pltpu.VMEM((nctx * slots, hidden), F32),
        pltpu.VMEM((nctx * slots, hidden), BF16),
        pltpu.VMEM((chunks, nz * slots, block), BF16),
        pltpu.VMEM((chunks, nz * slots, block), BF16),
        pltpu.VMEM((chunks, nz * slots, block), F32),
        pltpu.VMEM((hold, nz, slots, wide), BF16),
        pltpu.VMEM((hold, slots, wide), BF16),
        pltpu.VMEM((hold // 2, nz, slots, block), BF16),
        pltpu.VMEM((hold // 2, nz, slots, block), BF16),
        pltpu.VMEM((nexp, nz, pack, wide), BF16),
        pltpu.VMEM((nexp, nz, pack, wide), BF16),
        pltpu.VMEM((nexp, pack, wide), BF16),
        pltpu.VMEM((nexp, pack, wide), BF16),
        pltpu.VMEM((nz, stacked, wide), BF16),
        pltpu.VMEM((nz, stacked, wide), BF16),
        dma((12,)),
        dma((2, chunks)),
        dma((2,)),
        dma((2, nctx)),
        dma((2, nctx)),
        dma((nz,)),
        dma((nz,)),
        dma((2, nz, nx)),
        dma((2, nz, nx)),
        dma((2, nz, nx)),
        dma((2, nz, nx)),
        dma((2, nz)),
        dma((nz,)),
        dma((nz,)),
        dma((nexp,)),
        dma((nexp,)),
        dma((2, nexp)),
        dma((2, nexp)),
        dma((2, nz)),
        dma((2, nz)),
        dma((2, nz)),
        dma((2, nz)),
        dma((2,)),
        dma((2,)),
        dma((chunks,)),
        dma((chunks,)),
        dma((hold // 2, nz)),
        dma((hold // 2, nz)),
        dma((2, nexp)),
        dma((2, nexp)),
        dma((2, nz)),
    ]
    return pl.pallas_call(
        functools.partial(kernel, nctx, nexp),
        out_shape=jax.ShapeDtypeStruct((mine, width), BF16),
        in_specs=[pl.BlockSpec(memory_space=pl.ANY)] * len(operands),
        out_specs=pl.BlockSpec(memory_space=pltpu.VMEM),
        scratch_shapes=scratch,
        compiler_params=pltpu.CompilerParams(
            collective_id=0, has_side_effects=True, vmem_limit_bytes=60 * 2**20
        ),
    )(*operands)


def solution(mesh):
    return jax.shard_map(
        functools.partial(shards, mesh.shape["ctx"], mesh.shape["exp"]),
        mesh=mesh,
        in_specs=(
            P("ctx", "exp"),
            P("ctx", "exp"),
            P("ctx", "exp"),
            P("ctx", None),
            P("ctx", None),
            P("exp", None),
            P("exp"),
            P("exp", "ctx"),
            P(("ctx", "exp"), None),
            P(),
            P(("ctx", "exp"), None),
            P(("ctx", "exp"), None),
            P("exp", None, "ctx"),
            P("exp", "ctx", None),
        ),
        out_specs=P(("ctx", "exp"), None),
        check_vma=False,
    )
```

```python
import functools
import math

import jax
import jax.numpy as jnp
from jax import lax
from jax.experimental import pallas as pl
from jax.experimental.pallas import tpu as pltpu
from jax.sharding import PartitionSpec as P

MESH = pl.DeviceIdType.MESH
CAP = 2
EPSILON = 1e-05
LOG2E = math.log2(math.e)
F32 = jnp.float32
BF16 = jnp.bfloat16
STEPS = 16


def remote(src, dst, send_sem, recv_sem, device):
    return pltpu.make_async_remote_copy(
        src_ref=src,
        dst_ref=dst,
        send_sem=send_sem,
        recv_sem=recv_sem,
        device_id=device,
        device_id_type=MESH,
    )


def loop(count, body):
    def step(k, carry):
        body(k)
        return carry

    lax.fori_loop(0, count, step, 0)


def kernel(
    nctx,
    nexp,
    x_hbm,
    gate_hbm,
    step_hbm,
    write_hbm,
    read_hbm,
    rates_hbm,
    skip_hbm,
    ow_hbm,
    res_hbm,
    gain_hbm,
    ids_hbm,
    pairgate_hbm,
    up_hbm,
    down_hbm,
    out_ref,
    x_v,
    gate_v,
    step_v,
    write_v,
    read_v,
    rates_v,
    skip_v,
    res_v,
    gain_v,
    ids_v,
    pairgate_v,
    write_t,
    read_t,
    up_v,
    down_v,
    w_v,
    dt_f,
    u_f,
    wb_v,
    rb_v,
    rate2_v,
    h_v,
    hsend,
    hrecv,
    tsend,
    trecv,
    meta_v,
    metas,
    mixed_v,
    near_send,
    near_recv,
    far_send,
    far_recv,
    stream_v,
    table_v,
    gated_v,
    order_v,
    slot_v,
    nrows,
    lsend,
    lrecv,
    qsend,
    qrecv,
    rows_v,
    acc_v,
    lifted_v,
    osend,
    orecv,
    okeep,
    rsum,
    lsum,
    rsend,
    rrecv,
    qsend2,
    qrecv2,
    lsend2,
    lrecv2,
    csend,
    crecv,
    lsem,
    wsem,
    wswap,
    hs_sem,
    hr_sem,
    ms_sem,
    mr_sem,
    ps_sem,
    pr_sem,
    zs_sem,
    zr_sem,
    mt_sem,
    ns_sem,
    nr_sem,
    ls_sem,
    lr_sem,
    qs_sem,
    qr_sem,
    xs_sem,
    xr_sem,
    fs_sem,
    fr_sem,
    gs_sem,
    gr_sem,
    os_sem,
    or_sem,
    rs_sem,
    rr_sem,
    hq_sem,
    hl_sem,
    cs_sem,
):
    i = lax.axis_index("ctx")
    j = lax.axis_index("exp")
    nz = nctx // 2
    z = lax.div(i, 2)
    c = lax.rem(i, 2)
    nx = math.isqrt(nexp)
    y, x = lax.div(j, nx), lax.rem(j, nx)
    partner = (z * 2 + 1 - c, j)
    tokens, channels = x_hbm.shape
    states = write_hbm.shape[0]
    mine, width = res_hbm.shape
    block = width // nctx
    hidden = up_hbm.shape[1]
    chunks = nctx
    parts = 2 * chunks
    slots = nexp * CAP
    half = nz * slots

    def at_z(zz):
        return (zz * 2 + c, j)

    def at_e(e):
        return (i, e)

    def z_next(k):
        return lax.rem(z + k, nz)

    def e_next(k):
        return lax.rem(j + k, nexp)

    small = [
        (write_hbm, write_v),
        (read_hbm, read_v),
        (rates_hbm, rates_v),
        (step_hbm, step_v),
        (x_hbm, x_v),
        (gate_hbm, gate_v),
        (skip_hbm, skip_v),
        (res_hbm, res_v),
        (gain_hbm, gain_v),
        (ids_hbm, ids_v),
        (pairgate_hbm, pairgate_v),
        (ow_hbm, w_v.at[c]),
    ]
    small = [
        pltpu.make_async_copy(src, dst, lsem.at[n]) for n, (src, dst) in enumerate(small)
    ]
    for copy in small:
        copy.start()

    barrier = pltpu.get_barrier_semaphore()

    def greet_ctx(k):
        pl.semaphore_signal(
            barrier, inc=1, device_id=(lax.rem(i + k + 1, nctx), j), device_id_type=MESH
        )

    loop(nctx - 1, greet_ctx)
    for k in range(1, nx):
        for e in (y * nx + lax.rem(x + k, nx), lax.rem(y + k, nx) * nx + x):
            pl.semaphore_signal(barrier, inc=1, device_id=at_e(e), device_id_type=MESH)

    def up_copy(k):
        part = pl.ds(pl.multiple_of(k * block, block), block)
        return pltpu.make_async_copy(up_hbm.at[part], up_v.at[part], wsem.at[0, k])

    depth = hidden // chunks

    def down_copy(k):
        part = pl.ds(pl.multiple_of(k * depth, depth), depth)
        return pltpu.make_async_copy(down_hbm.at[part], down_v.at[part], wsem.at[1, k])

    loop(chunks, lambda k: up_copy(k).start())
    loop(chunks, lambda k: down_copy(k).start())

    small[0].wait()
    small[1].wait()
    write_t[...] = write_v[...].T
    read_t[...] = read_v[...].T
    diagonal = lax.broadcasted_iota(jnp.int32, (1, states, states), 1) == lax.broadcasted_iota(
        jnp.int32, (1, states, states), 2
    )

    def spread(n):
        part = pl.ds(pl.multiple_of(n * STEPS, STEPS), STEPS)
        for source, wide in ((write_t, wb_v), (read_t, rb_v)):
            rows = jnp.broadcast_to(source[part, :][:, None, :], (STEPS, states, states))
            picked = jnp.sum(jnp.where(diagonal, rows, 0.0), axis=2, keepdims=True)
            wide[part] = jnp.broadcast_to(picked, (STEPS, states, 128))

    loop(tokens // STEPS, spread)
    small[2].wait()
    rate2_v[...] = rates_v[...] * (-LOG2E)
    small[3].wait()
    small[4].wait()

    def widen(n):
        part = pl.ds(pl.multiple_of(n * STEPS, STEPS), STEPS)
        steps = step_v[part, :].astype(F32)
        dt_f[part, :] = steps
        u_f[part, :] = steps * x_v[part, :].astype(F32)

    loop(tokens // STEPS, widen)
    copies = channels // 128

    def advance(h, t, rate2):
        decay = jnp.exp2(dt_f[pl.ds(t, 1), :] * rate2)
        push = u_f[pl.ds(t, 1), :] * jnp.concatenate([wb_v[t]] * copies, axis=1)
        return decay * h + push

    def first(n, carry):
        h, total = carry
        rate2 = rate2_v[...]
        for r in range(STEPS):
            h = advance(h, n * STEPS + r, rate2)
        part = pl.ds(pl.multiple_of(n * STEPS, STEPS), STEPS)
        return h, total + jnp.sum(dt_f[part, :], axis=0, keepdims=True)

    h, total = lax.fori_loop(
        0,
        tokens // STEPS,
        first,
        (jnp.zeros((states, channels), F32), jnp.zeros((1, channels), F32)),
    )
    hsend[...] = h.astype(BF16)
    folded = jnp.concatenate([total[:, q * 128 : (q + 1) * 128] for q in range(copies)], axis=0)
    tsend[...] = jnp.concatenate([folded] * (8 // copies), axis=0)
    meta_v[...] = jnp.zeros_like(meta_v)
    small[9].wait()
    small[10].wait()
    meta_v[0:2, 0:mine] = ids_v[...].astype(F32)
    meta_v[2:4, 0:mine] = pairgate_v[...].astype(F32)

    wide = width // parts
    hold = parts // 2
    pack = hold * CAP
    stacked = hold * mine
    places = nexp * pack
    lanes = lax.broadcasted_iota(jnp.int32, (mine, 128), 1)
    square = lax.broadcasted_iota(jnp.int32, (mine, mine), 0) == lax.broadcasted_iota(
        jnp.int32, (mine, mine), 1
    )
    earlier = (
        lax.broadcasted_iota(jnp.int32, (mine, mine), 0)
        > lax.broadcasted_iota(jnp.int32, (mine, mine), 1)
    ).astype(F32)
    column = lax.broadcasted_iota(jnp.int32, (stacked, places), 1)
    row = lax.broadcasted_iota(jnp.int32, (stacked, places), 0)
    column_slot = lax.div(column, pack) * CAP + lax.rem(column, CAP)
    same_part = lax.rem(lax.div(column, CAP), hold) == lax.div(row, mine)
    slot_v[...] = jnp.where(same_part, column_slot, -1)

    source = lax.broadcasted_iota(jnp.int32, (places, places), 1)
    target = lax.broadcasted_iota(jnp.int32, (places, places), 0)

    def by_part(index):
        return (
            lax.rem(lax.div(index, CAP), hold) * slots
            + lax.div(index, pack) * CAP
            + lax.rem(index, CAP)
        )

    order_v[0] = (by_part(source) == target).astype(F32).astype(BF16)
    order_v[1] = (by_part(target) == source).astype(F32).astype(BF16)

    pl.semaphore_wait(barrier, nctx - 1 + 2 * (nx - 1))

    def state_copies(k):
        device = (lax.rem(i + k, nctx), j)
        return (
            remote(tsend, trecv.at[i], hs_sem.at[0, k], hr_sem.at[0, i], device),
            remote(hsend, hrecv.at[i], hs_sem.at[1, k], hr_sem.at[1, i], device),
        )

    for k in range(1, nctx):

        @pl.when(i + k < nctx)
        def _():
            for copy in state_copies(k):
                copy.start()

    def drain_states():
        for k in range(1, nctx):

            @pl.when(i + k < nctx)
            def _():
                for copy in state_copies(k):
                    copy.wait_send()

    sent = [drain_states]

    def meta_copy(k):
        return remote(
            meta_v, metas.at[z], mt_sem.at[0, k], mt_sem.at[1, z], at_z(z_next(k))
        )

    small[11].wait()
    swap = remote(w_v.at[c], w_v.at[c], wswap.at[0], wswap.at[1], partner)
    swap.start()
    sent.append(swap.wait_send)

    h_v[...] = jnp.zeros_like(h_v)
    for k in range(nctx - 1):

        @pl.when(k < i)
        def _():
            remote(tsend, trecv.at[k], hs_sem.at[0, 0], hr_sem.at[0, k], partner).wait_recv()
            remote(hsend, hrecv.at[k], hs_sem.at[1, 0], hr_sem.at[1, k], partner).wait_recv()
            passed = jnp.concatenate([trecv[k, q : q + 1, :] for q in range(copies)], axis=1)
            h_v[...] = jnp.exp2(rate2_v[...] * passed) * h_v[...] + hrecv[k].astype(F32)

    for k in range(1, nz):
        meta_copy(k).start()
    metas[z] = meta_v[...]
    sent.append(lambda: [meta_copy(k).wait_send() for k in range(1, nz)])

    small[5].wait()
    small[6].wait()

    def second(n, h):
        part = pl.ds(pl.multiple_of(n * STEPS, STEPS), STEPS)
        rate2 = rate2_v[...]
        reads = []
        for r in range(STEPS):
            t = n * STEPS + r
            h = advance(h, t, rate2)
            seen = h * jnp.concatenate([rb_v[t]] * copies, axis=1)
            reads.append(jnp.sum(seen, axis=0, keepdims=True))
        readout = jnp.concatenate(reads, axis=0)
        readout = readout + skip_v[...] * x_v[part, :].astype(F32)
        gate = gate_v[part, :].astype(F32)
        mixed_v[z, part, :] = (readout * (gate / (1.0 + jnp.exp(-gate)))).astype(BF16)
        return h

    reach = (1, nz - 1) if nz > 2 else (1,)
    beyond = tuple(range(2, nz - 1))

    def mixed_copy(n, k):
        part = mixed_v.at[z, n * (tokens // 2) : (n + 1) * (tokens // 2)]
        return remote(part, part, ms_sem.at[n, k], mr_sem.at[n, z], at_z(z_next(k)))

    def mixed_arrive(zz):
        for n in range(2):
            part = mixed_v.at[zz, n * (tokens // 2) : (n + 1) * (tokens // 2)]
            remote(part, part, ms_sem.at[n, 0], mr_sem.at[n, zz], partner).wait_recv()

    turns = tokens // STEPS // 2
    h = h_v[...]
    for n in range(2):
        h = lax.fori_loop(n * turns, (n + 1) * turns, second, h)
        for k in reach:
            mixed_copy(n, k).start()
    for n in range(2):
        for k in beyond:
            mixed_copy(n, k).start()
    sent.append(lambda: [mixed_copy(n, k).wait_send() for k in reach + beyond for n in range(2)])

    swap.wait_recv()

    def line(side, n):
        return at_e(y * nx + n) if side == 0 else at_e(n * nx + x)

    def line_of(side):
        return x if side == 0 else y

    def line_next(side, k):
        return lax.rem(line_of(side) + k, nx)

    def near_copy(side, zz, k):
        n = line_next(side, k)
        return remote(
            near_send.at[side, zz, n],
            near_recv.at[side, zz, line_of(side)],
            ps_sem.at[side, zz, k],
            pr_sem.at[side, zz, line_of(side)],
            line(side, n),
        )

    def farthest_last(k):
        return k + lax.div(k, 2) * (5 - 2 * k) if nz == 4 else k

    def project(k):
        zz = z_next(farthest_last(k))

        @pl.when(k > 0)
        def _():
            mixed_arrive(zz)

        for side in range(2):
            part = jnp.dot(mixed_v[zz], w_v[side], preferred_element_type=F32)
            part = part.reshape(nx, nx, mine, block)
            if side == 0:
                part = jnp.stack(
                    [
                        jnp.concatenate([part[b, a] for b in range(nx)], axis=0)
                        for a in range(nx)
                    ]
                )
            near_send[side, zz] = part.reshape(nx, nx * mine, block).astype(BF16)
            for n in range(1, nx):
                near_copy(side, zz, n).start()
            near_recv[side, zz, line_of(side)] = near_send[side, zz, line_of(side)]

    sent.append(
        lambda: loop(
            nz,
            lambda zz: [
                near_copy(side, zz, n).wait_send() for side in range(2) for n in range(1, nx)
            ],
        )
    )

    def far_line(side, zz, n):
        if side == 0:
            return (zz * 2 + c, n * nx + x)
        return (zz * 2 + c, y * nx + n)

    def far_copy(side, zz, k):
        n = line_next(1 - side, k)
        return remote(
            far_send.at[side, zz, n],
            far_recv.at[side, z, line_of(1 - side)],
            zs_sem.at[side, zz, k],
            zr_sem.at[side, z, line_of(1 - side)],
            far_line(side, zz, n),
        )

    def far_out(k):
        zz = z_next(farthest_last(k))
        for side in range(2):
            for n in range(1, nx):
                m = line_next(side, n)
                remote(
                    near_send.at[side, zz, m],
                    near_recv.at[side, zz, m],
                    ps_sem.at[side, zz, 0],
                    pr_sem.at[side, zz, m],
                    partner,
                ).wait_recv()
            part = near_recv[side, zz, 0].astype(F32)
            for n in range(1, nx):
                part = part + near_recv[side, zz, n].astype(F32)
            part = part.reshape(nx, mine, block)
            part = jnp.concatenate([part[:, :, : block // 2], part[:, :, block // 2 :]], axis=1)
            far_send[side, zz] = part.astype(BF16)

            @pl.when(k == 0)
            def _():
                me = line_of(1 - side)
                far_recv[side, zz, me] = far_send[side, zz, me]

            @pl.when(k > 0)
            def _():
                far_copy(side, zz, 0).start()

            for n in range(1, nx):
                far_copy(side, zz, n).start()

    project(0)
    def column_of(values):
        return jnp.sum(jnp.where(square, values, 0.0), axis=1, keepdims=True)

    def tables(zz):
        meta = metas[zz]
        idents = [column_of(meta[n : n + 1, 0:mine]).astype(jnp.int32) for n in range(2)]
        hots = [(lanes == ident).astype(F32) for ident in idents]
        before = jnp.dot(earlier, hots[0] + hots[1], preferred_element_type=F32)
        table = jnp.zeros((stacked, places), F32)
        gated = jnp.zeros((stacked, places), F32)
        for n in range(2):
            rank = jnp.sum(before * hots[n], axis=1, keepdims=True).astype(jnp.int32)
            slot = jnp.concatenate([idents[n] * CAP + rank] * hold, axis=0)
            taken = jnp.where(slot_v[...] == slot, 1.0, 0.0)
            weight = column_of(meta[n + 2 : n + 3, 0:mine])
            table = table + taken
            gated = gated + taken * jnp.concatenate([weight] * hold, axis=0)
        gated_v[zz] = gated.astype(BF16)
        table_v[zz] = table.T.astype(BF16)

    tables(z)

    def other_tables(k):
        zz = z_next(k + 1)
        remote(meta_v, metas.at[zz], mt_sem.at[0, 0], mt_sem.at[1, zz], partner).wait_recv()
        tables(zz)

    loop(nz - 1, other_tables)
    far_out(0)
    loop(nz - 1, lambda k: project(k + 1))
    loop(nz - 1, lambda k: far_out(k + 1))

    def drain_far():
        for side in range(2):
            for k in range(nz):
                for n in range(0 if k else 1, nx):
                    far_copy(side, z_next(k), n).wait_send()

    sent.append(drain_far)

    def stack(wide_rows):
        return jnp.concatenate(
            [wide_rows[:, k * wide : (k + 1) * wide] for k in range(parts)], axis=0
        )

    small[7].wait()
    small[8].wait()
    res = stack(res_v[...].astype(F32))
    gain = stack(jnp.broadcast_to(gain_v[...], (mine, width)))
    for side in range(2):
        for k in range(nz):
            for n in range(0 if k else 1, nx):
                zz, m = z_next(k), line_next(1 - side, n)
                remote(
                    far_send.at[side, zz, m],
                    far_recv.at[side, zz, m],
                    zs_sem.at[side, zz, 0],
                    zr_sem.at[side, zz, m],
                    partner,
                ).wait_recv()
    summed_parts = []
    for zz in range(nz):
        for side in range(2):
            part = far_recv[side, zz, 0].astype(F32)
            for n in range(1, nx):
                part = part + far_recv[side, zz, n].astype(F32)
            summed_parts.append(part)
    stream = (res + jnp.concatenate(summed_parts, axis=0)).astype(BF16).astype(F32)
    stream_v[...] = stream
    squares = jnp.sum(stream * stream, axis=1, keepdims=True).reshape(parts, mine, 1)
    scale = lax.rsqrt(jnp.sum(squares, axis=0) / width + EPSILON)
    normed = (stream * jnp.concatenate([scale] * parts, axis=0) * gain).astype(BF16)

    nrows[z] = normed[stacked:]

    def norm_copy(k):
        return remote(nrows.at[z], nrows.at[z], ns_sem.at[k], nr_sem.at[z], at_z(z_next(k)))

    for k in range(1, nz):
        norm_copy(k).start()
    sent.append(lambda: [norm_copy(k).wait_send() for k in range(1, nz)])

    def slotted(zz, rows):
        return (
            jnp.dot(table_v[zz], rows, preferred_element_type=F32)
            .astype(BF16)
            .reshape(nexp, pack, wide)
        )

    def left_copy(k):
        e = e_next(k)
        return remote(lsend.at[e], lrecv.at[j], ls_sem.at[k], lr_sem.at[j], at_e(e))

    lsend[...] = slotted(z, normed[:stacked])
    loop(nexp - 1, lambda k: left_copy(k + 1).start())
    lrecv[j] = lsend[j]
    sent.append(lambda: loop(nexp - 1, lambda k: left_copy(k + 1).wait_send()))

    def right_copy(k):
        e = e_next(k)
        return remote(qsend.at[e], qrecv.at[j], qs_sem.at[0, k], qr_sem.at[0, j], at_e(e))

    qsend[:, 0] = slotted(z, normed[stacked:])

    def right_out():
        def right_slots(k):
            zz = z_next(k + 1)
            remote(nrows.at[zz], nrows.at[zz], ns_sem.at[0], nr_sem.at[zz], partner).wait_recv()
            qsend[:, k + 1] = slotted(zz, nrows[zz])

        loop(nz - 1, right_slots)
        loop(nexp - 1, lambda k: right_copy(k + 1).start())
        qrecv[j] = qsend[j]
        sent.append(lambda: loop(nexp - 1, lambda k: right_copy(k + 1).wait_send()))

    def left_arrive(k):
        e = e_next(k + 1)
        remote(lsend.at[e], lrecv.at[e], ls_sem.at[0], lr_sem.at[e], partner).wait_recv()

    def rows_part(zz):
        return pl.ds(pl.multiple_of(zz * slots, slots), slots)

    def arranged(rows):
        return (
            jnp.dot(order_v[0], rows.reshape(places, wide), preferred_element_type=F32)
            .astype(BF16)
            .reshape(hold, slots, wide)
        )

    def rows_copy(g, n):
        here = rows_v.at[pl.ds(g * group, group), rows_part(z)]
        return remote(here, here, xs_sem.at[g, n], xr_sem.at[g, z], at_z(z_next(n)))

    def forward_copy(g, zz):
        return remote(
            rows_v.at[pl.ds(g * group, group), rows_part(zz)],
            rows_v.at[pl.ds(g * group, group), pl.ds(pl.multiple_of(half + zz * slots, slots), slots)],
            fs_sem.at[g, zz],
            fr_sem.at[g, zz],
            partner,
        )

    def right_forward(g):
        at = pl.ds(hold + g * group, group)
        return remote(
            rows_v.at[at, pl.ds(0, half)],
            rows_v.at[at, pl.ds(half, half)],
            gs_sem.at[g],
            gr_sem.at[g],
            partner,
        )

    group = hold // 2
    loop(nexp - 1, left_arrive)
    rows_v[0:hold, rows_part(z), :] = arranged(lrecv[...])
    for g in range(2):
        for n in range(1, nz):
            rows_copy(g, n).start()
        forward_copy(g, z).start()

    right_out()

    def right_arrive():
        def one(k):
            e = e_next(k + 1)
            remote(qsend.at[e], qrecv.at[e], qs_sem.at[0, 0], qr_sem.at[0, e], partner).wait_recv()

        loop(nexp - 1, one)

    def right_rows(k):
        rows_v[hold:parts, rows_part(z_next(k)), :] = arranged(qrecv[:, k])

    tile = 512 if hidden % 512 == 0 else hidden
    tiles = hidden // tile

    def tile_columns(n):
        return pl.ds(pl.multiple_of(n * tile, tile), tile)

    def product(start, count, columns):
        rows = jnp.concatenate([rows_v[start + k] for k in range(count)], axis=1)
        weights = up_v[start * wide : (start + count) * wide, columns]
        return jnp.dot(rows, weights, preferred_element_type=F32)

    def group_arrive(g):
        for n in range(1, nz):
            zz = z_next(farthest_last(n))
            there = rows_v.at[pl.ds(g * group, group), rows_part(zz)]
            remote(there, there, xs_sem.at[g, 0], xr_sem.at[g, zz], partner).wait_recv()
            forward_copy(g, zz).start()

    def group_forwarded(g):
        for zz in range(nz):
            forward_copy(g, zz).wait_recv()

    group_arrive(0)
    loop(chunks, lambda k: up_copy(k).wait())
    group_forwarded(0)

    def lift_first(n):
        columns = tile_columns(n)
        acc_v[:, columns] = product(0, group, columns)

    loop(tiles, lift_first)
    group_arrive(1)
    right_arrive()
    loop(nz, right_rows)
    for g in range(2):
        right_forward(g).start()

    def drain_rows():
        for g in range(2):
            right_forward(g).wait_send()
            for n in range(1, nz):
                rows_copy(g, n).wait_send()
            for zz in range(nz):
                forward_copy(g, zz).wait_send()

    sent.append(drain_rows)
    group_forwarded(1)

    def lift_second(n):
        columns = tile_columns(n)
        acc_v[:, columns] += product(group, group, columns)

    loop(tiles, lift_second)
    for g in range(2):
        right_forward(g).wait_recv()

    def lift_right(n):
        columns = tile_columns(n)
        lifted = acc_v[:, columns] + product(hold, hold, columns)
        lifted_v[:, columns] = (lifted / (1.0 + jnp.exp(-lifted))).astype(BF16)

    loop(tiles, lift_right)
    loop(chunks, lambda k: down_copy(k).wait())

    halves = chunks // 2

    def step_of(k):
        return lax.rem(k + halves, chunks)

    def pair_copy(k):
        return remote(osend.at[k], orecv.at[k], os_sem.at[k], or_sem.at[k], partner)

    def lower(n):
        k = step_of(n)
        columns = pl.ds(pl.multiple_of(k * block, block), block)
        product = jnp.dot(lifted_v[...], down_v[:, columns], preferred_element_type=F32)
        okeep[k] = product[0:half]
        osend[k] = product[half : 2 * half].astype(BF16)
        pair_copy(k).start()

    def paired(k):
        pair_copy(k).wait_recv()
        return okeep[k] + orecv[k].astype(F32)

    def keep_right(n):
        both = paired(halves + n).astype(BF16)
        for q in range(2):
            rsum[2 * n + q] = both[:, q * wide : (q + 1) * wide].reshape(nz, slots, wide)

    def back_copy(k, n):
        zz = z_next(n)
        return remote(
            rsend.at[k, zz], rrecv.at[k, z], rs_sem.at[k, n], rr_sem.at[k, z], at_z(zz)
        )

    def send_back(k):
        rsend[k] = paired(k).astype(BF16).reshape(nz, slots, block)
        for n in range(1, nz):
            back_copy(k, n).start()
        rrecv[k, z] = rsend[k, z]

    ahead = halves // 2
    loop(ahead, lambda n: lower(halves + n))
    for n in range(halves):
        lower(n)
    loop(ahead, send_back)
    loop(halves - 1, keep_right)
    lower(halves + ahead)
    keep_right(halves - 1)

    def unarranged(rows):
        return (
            jnp.dot(order_v[1], rows.reshape(places, wide), preferred_element_type=F32)
            .astype(BF16)
            .reshape(nexp, pack, wide)
        )

    def home_right_copy(k, first):
        e = e_next(k)
        which = pl.ds(1, nz - 1) if first else pl.ds(0, 1)
        n = 0 if first else 1
        return remote(
            qsend2.at[e, which],
            qrecv2.at[j, which],
            hq_sem.at[0, n, k],
            hq_sem.at[1, n, j],
            at_e(e),
        )

    def home_right(k):
        qsend2[:, k] = unarranged(rsum[:, z_next(k)])

    loop(nz - 1, lambda k: home_right(k + 1))
    loop(nexp - 1, lambda k: home_right_copy(k + 1, True).start())
    home_right(0)
    loop(nexp - 1, lambda k: home_right_copy(k + 1, False).start())
    qrecv2[j] = qsend2[j]
    sent.append(
        lambda: loop(
            nexp - 1,
            lambda k: [home_right_copy(k + 1, first).wait_send() for first in (True, False)],
        )
    )

    loop(halves - ahead - 1, lambda n: lower(n + halves + ahead + 1))
    loop(halves - ahead, lambda n: send_back(n + ahead))

    def drain_back(k):
        for n in range(1, nz):
            back_copy(k, n).wait_send()

    sent.append(lambda: loop(halves, drain_back))
    sent.append(lambda: loop(chunks, lambda k: pair_copy(k).wait_send()))

    def back_arrive(k):
        for n in range(1, nz):
            zz = z_next(n)
            remote(
                rsend.at[k, zz], rrecv.at[k, zz], rs_sem.at[k, 0], rr_sem.at[k, zz], partner
            ).wait_recv()
        total = rrecv[k, 0].astype(F32)
        for zz in range(1, nz):
            total = total + rrecv[k, zz].astype(F32)
        for q in range(2):
            lsum[2 * k + q] = total[:, q * wide : (q + 1) * wide].astype(BF16)

    loop(halves, back_arrive)
    lsend2[...] = unarranged(lsum[...])

    def home_left_copy(k):
        e = e_next(k)
        return remote(lsend2.at[e], lrecv2.at[j], hl_sem.at[0, k], hl_sem.at[1, j], at_e(e))

    loop(nexp - 1, lambda k: home_left_copy(k + 1).start())
    lrecv2[j] = lsend2[j]
    sent.append(lambda: loop(nexp - 1, lambda k: home_left_copy(k + 1).wait_send()))

    def home_right_arrive(n):
        which = pl.ds(1, nz - 1) if n == 0 else pl.ds(0, 1)

        def one(k):
            e = e_next(k + 1)
            remote(
                qsend2.at[e, which],
                qrecv2.at[e, which],
                hq_sem.at[0, n, 0],
                hq_sem.at[1, n, e],
                partner,
            ).wait_recv()

        loop(nexp - 1, one)

    home_right_arrive(0)

    def weighed(zz, rows):
        return jnp.dot(gated_v[zz], rows.reshape(places, wide), preferred_element_type=F32)

    def token_copy(k):
        zz = z_next(k)
        return remote(csend.at[zz], crecv.at[z], cs_sem.at[0, k], cs_sem.at[1, z], at_z(zz))

    for n in range(1, nz):
        k = n + n // 2 * (5 - 2 * n) if nz == 4 else n
        zz = z_next(k)
        csend[zz] = weighed(zz, qrecv2[:, k]).astype(BF16)
        token_copy(k).start()
    home_right_arrive(1)
    crecv[z] = weighed(z, qrecv2[:, 0]).astype(BF16)
    sent.append(lambda: [token_copy(k).wait_send() for k in range(1, nz)])

    def home_left_arrive(k):
        e = e_next(k + 1)
        remote(
            lsend2.at[e], lrecv2.at[e], hl_sem.at[0, 0], hl_sem.at[1, e], partner
        ).wait_recv()

    def give(first, rows):
        for k in range(hold):
            at = (0 if first else hold) + k
            out_ref[:, at * wide : (at + 1) * wide] = rows[k * mine : (k + 1) * mine].astype(BF16)

    loop(nexp - 1, home_left_arrive)
    give(True, stream_v[0:stacked] + weighed(z, lrecv2[...]))
    for k in range(1, nz):
        zz = z_next(k)
        remote(
            csend.at[zz], crecv.at[zz], cs_sem.at[0, 0], cs_sem.at[1, zz], partner
        ).wait_recv()
    total = stream_v[stacked : 2 * stacked]
    for zz in range(nz):
        total = total + crecv[zz].astype(F32)
    give(False, total)

    for drain in sent:
        drain()


def shards(nctx, nexp, *arrays):
    (
        mixer_input,
        mixer_gate,
        step_size,
        write_coeffs,
        read_coeffs,
        decay_rates,
        skip_scale,
        out_weight,
        residual_in,
        norm_gain,
        expert_ids,
        gate_weights,
        up_weight,
        down_weight,
    ) = arrays
    tokens, channels = mixer_input.shape
    states = write_coeffs.shape[1]
    mine, width = residual_in.shape
    hidden = up_weight.shape[2]
    nz = nctx // 2
    nx = math.isqrt(nexp)
    block = width // nctx
    chunks = nctx
    slots = nexp * CAP
    parts = 2 * chunks
    wide = width // parts
    hold = parts // 2
    pack = hold * CAP
    stacked = hold * mine
    places = nexp * pack
    operands = (
        mixer_input,
        mixer_gate,
        step_size,
        write_coeffs.T,
        read_coeffs.T,
        decay_rates.T,
        skip_scale.reshape(1, channels),
        out_weight,
        residual_in,
        norm_gain.reshape(1, width),
        expert_ids.T,
        gate_weights.T,
        up_weight.reshape(width, hidden),
        down_weight.reshape(hidden, width),
    )
    dma = pltpu.SemaphoreType.DMA
    scratch = [
        pltpu.VMEM((tokens, channels), BF16),
        pltpu.VMEM((tokens, channels), BF16),
        pltpu.VMEM((tokens, channels), BF16),
        pltpu.VMEM((states, tokens), F32),
        pltpu.VMEM((states, tokens), F32),
        pltpu.VMEM((states, channels), F32),
        pltpu.VMEM((1, channels), F32),
        pltpu.VMEM((mine, width), BF16),
        pltpu.VMEM((1, width), F32),
        pltpu.VMEM((2, mine), jnp.int32),
        pltpu.VMEM((2, mine), BF16),
        pltpu.VMEM((tokens, states), F32),
        pltpu.VMEM((tokens, states), F32),
        pltpu.VMEM((width, hidden), BF16),
        pltpu.VMEM((hidden, width), BF16),
        pltpu.VMEM((2, channels, block), BF16),
        pltpu.VMEM((tokens, channels), F32),
        pltpu.VMEM((tokens, channels), F32),
        pltpu.VMEM((tokens, states, 128), F32),
        pltpu.VMEM((tokens, states, 128), F32),
        pltpu.VMEM((states, channels), F32),
        pltpu.VMEM((states, channels), F32),
        pltpu.VMEM((states, channels), BF16),
        pltpu.VMEM((nctx, states, channels), BF16),
        pltpu.VMEM((8, 128), F32),
        pltpu.VMEM((nctx, 8, 128), F32),
        pltpu.VMEM((8, 128), F32),
        pltpu.VMEM((nz, 8, 128), F32),
        pltpu.VMEM((nz, tokens, channels), BF16),
        pltpu.VMEM((2, nz, nx, nx * mine, block), BF16),
        pltpu.VMEM((2, nz, nx, nx * mine, block), BF16),
        pltpu.VMEM((2, nz, nx, 2 * mine, wide), BF16),
        pltpu.VMEM((2, nz, nx, 2 * mine, wide), BF16),
        pltpu.VMEM((parts * mine, wide), F32),
        pltpu.VMEM((nz, places, stacked), BF16),
        pltpu.VMEM((nz, stacked, places), BF16),
        pltpu.VMEM((2, places, places), BF16),
        pltpu.VMEM((stacked, places), jnp.int32),
        pltpu.VMEM((nz, stacked, wide), BF16),
        pltpu.VMEM((nexp, pack, wide), BF16),
        pltpu.VMEM((nexp, pack, wide), BF16),
        pltpu.VMEM((nexp, nz, pack, wide), BF16),
        pltpu.VMEM((nexp, nz, pack, wide), BF16),
        pltpu.VMEM((parts, nctx * slots, wide), BF16),
        pltpu.VMEM((nctx * slots, hidden), F32),
        pltpu.VMEM((nctx * slots, hidden), BF16),
        pltpu.VMEM((chunks, nz * slots, block), BF16),
        pltpu.VMEM((chunks, nz * slots, block), BF16),
        pltpu.VMEM((chunks, nz * slots, block), F32),
        pltpu.VMEM((hold, nz, slots, wide), BF16),
        pltpu.VMEM((hold, slots, wide), BF16),
        pltpu.VMEM((hold // 2, nz, slots, block), BF16),
        pltpu.VMEM((hold // 2, nz, slots, block), BF16),
        pltpu.VMEM((nexp, nz, pack, wide), BF16),
        pltpu.VMEM((nexp, nz, pack, wide), BF16),
        pltpu.VMEM((nexp, pack, wide), BF16),
        pltpu.VMEM((nexp, pack, wide), BF16),
        pltpu.VMEM((nz, stacked, wide), BF16),
        pltpu.VMEM((nz, stacked, wide), BF16),
        dma((12,)),
        dma((2, chunks)),
        dma((2,)),
        dma((2, nctx)),
        dma((2, nctx)),
        dma((2, nz)),
        dma((2, nz)),
        dma((2, nz, nx)),
        dma((2, nz, nx)),
        dma((2, nz, nx)),
        dma((2, nz, nx)),
        dma((2, nz)),
        dma((nz,)),
        dma((nz,)),
        dma((nexp,)),
        dma((nexp,)),
        dma((2, nexp)),
        dma((2, nexp)),
        dma((2, nz)),
        dma((2, nz)),
        dma((2, nz)),
        dma((2, nz)),
        dma((2,)),
        dma((2,)),
        dma((chunks,)),
        dma((chunks,)),
        dma((hold // 2, nz)),
        dma((hold // 2, nz)),
        dma((2, 2, nexp)),
        dma((2, nexp)),
        dma((2, nz)),
    ]
    return pl.pallas_call(
        functools.partial(kernel, nctx, nexp),
        out_shape=jax.ShapeDtypeStruct((mine, width), BF16),
        in_specs=[pl.BlockSpec(memory_space=pl.ANY)] * len(operands),
        out_specs=pl.BlockSpec(memory_space=pltpu.VMEM),
        scratch_shapes=scratch,
        compiler_params=pltpu.CompilerParams(
            collective_id=0, has_side_effects=True, vmem_limit_bytes=60 * 2**20
        ),
    )(*operands)


def solution(mesh):
    return jax.shard_map(
        functools.partial(shards, mesh.shape["ctx"], mesh.shape["exp"]),
        mesh=mesh,
        in_specs=(
            P("ctx", "exp"),
            P("ctx", "exp"),
            P("ctx", "exp"),
            P("ctx", None),
            P("ctx", None),
            P("exp", None),
            P("exp"),
            P("exp", "ctx"),
            P(("ctx", "exp"), None),
            P(),
            P(("ctx", "exp"), None),
            P(("ctx", "exp"), None),
            P("exp", None, "ctx"),
            P("exp", "ctx", None),
        ),
        out_specs=P(("ctx", "exp"), None),
        check_vma=False,
    )
```

```python
import functools
import math

import jax
import jax.numpy as jnp
from jax import lax
from jax.experimental import pallas as pl
from jax.experimental.pallas import tpu as pltpu
from jax.sharding import PartitionSpec as P

MESH = pl.DeviceIdType.MESH
CAP = 2
EPSILON = 1e-05
LOG2E = math.log2(math.e)
F32 = jnp.float32
BF16 = jnp.bfloat16
STEPS = 16


def remote(src, dst, send_sem, recv_sem, device):
    return pltpu.make_async_remote_copy(
        src_ref=src,
        dst_ref=dst,
        send_sem=send_sem,
        recv_sem=recv_sem,
        device_id=device,
        device_id_type=MESH,
    )


def loop(count, body):
    def step(k, carry):
        body(k)
        return carry

    lax.fori_loop(0, count, step, 0)


def burst(count, body):
    for k in range(count):
        body(k)


def kernel(
    nctx,
    nexp,
    x_hbm,
    gate_hbm,
    step_hbm,
    write_hbm,
    read_hbm,
    rates_hbm,
    skip_hbm,
    ow_hbm,
    res_hbm,
    gain_hbm,
    ids_hbm,
    pairgate_hbm,
    up_hbm,
    down_hbm,
    out_ref,
    x_v,
    gate_v,
    step_v,
    write_v,
    read_v,
    rates_v,
    skip_v,
    res_v,
    gain_v,
    ids_v,
    pairgate_v,
    write_t,
    read_t,
    up_v,
    down_v,
    w_v,
    dt_f,
    u_f,
    wb_v,
    rb_v,
    rate2_v,
    h_v,
    hsend,
    hrecv,
    tsend,
    trecv,
    meta_v,
    metas,
    mixed_v,
    near_send,
    near_recv,
    far_send,
    far_recv,
    stream_v,
    table_v,
    gated_v,
    order_v,
    slot_v,
    nrows,
    lsend,
    lrecv,
    qsend,
    qrecv,
    rows_v,
    acc_v,
    lifted_v,
    osend,
    orecv,
    okeep,
    rsum,
    lsum,
    rsend,
    rrecv,
    qsend2,
    qrecv2,
    lsend2,
    lrecv2,
    csend,
    crecv,
    lsem,
    wsem,
    wswap,
    hs_sem,
    hr_sem,
    ms_sem,
    mr_sem,
    ps_sem,
    pr_sem,
    zs_sem,
    zr_sem,
    mt_sem,
    ns_sem,
    nr_sem,
    ls_sem,
    lr_sem,
    qs_sem,
    qr_sem,
    xs_sem,
    xr_sem,
    fs_sem,
    fr_sem,
    gs_sem,
    gr_sem,
    os_sem,
    or_sem,
    rs_sem,
    rr_sem,
    hq_sem,
    hl_sem,
    cs_sem,
):
    i = lax.axis_index("ctx")
    j = lax.axis_index("exp")
    nz = nctx // 2
    z = lax.div(i, 2)
    c = lax.rem(i, 2)
    nx = math.isqrt(nexp)
    y, x = lax.div(j, nx), lax.rem(j, nx)
    partner = (z * 2 + 1 - c, j)
    tokens, channels = x_hbm.shape
    states = write_hbm.shape[0]
    mine, width = res_hbm.shape
    block = width // nctx
    hidden = up_hbm.shape[1]
    chunks = nctx
    parts = 2 * chunks
    slots = nexp * CAP
    half = nz * slots

    def at_z(zz):
        return (zz * 2 + c, j)

    def at_e(e):
        return (i, e)

    def z_next(k):
        return lax.rem(z + k, nz)

    def e_next(k):
        return lax.rem(j + k, nexp)

    barrier = pltpu.get_barrier_semaphore()

    def greet_ctx(k):
        pl.semaphore_signal(
            barrier, inc=1, device_id=(lax.rem(i + k + 1, nctx), j), device_id_type=MESH
        )

    loop(nctx - 1, greet_ctx)
    for k in range(1, nx):
        for e in (y * nx + lax.rem(x + k, nx), lax.rem(y + k, nx) * nx + x):
            pl.semaphore_signal(barrier, inc=1, device_id=at_e(e), device_id_type=MESH)

    small = [
        (write_hbm, write_v),
        (read_hbm, read_v),
        (rates_hbm, rates_v),
        (step_hbm, step_v),
        (x_hbm, x_v),
        (gate_hbm, gate_v),
        (skip_hbm, skip_v),
        (res_hbm, res_v),
        (gain_hbm, gain_v),
        (ids_hbm, ids_v),
        (pairgate_hbm, pairgate_v),
        (ow_hbm, w_v.at[c]),
    ]
    small = [
        pltpu.make_async_copy(src, dst, lsem.at[n]) for n, (src, dst) in enumerate(small)
    ]
    for copy in small:
        copy.start()

    def up_copy(k):
        part = pl.ds(pl.multiple_of(k * block, block), block)
        return pltpu.make_async_copy(up_hbm.at[part], up_v.at[part], wsem.at[0, k])

    depth = hidden // chunks

    def down_copy(k):
        part = pl.ds(pl.multiple_of(k * depth, depth), depth)
        return pltpu.make_async_copy(down_hbm.at[part], down_v.at[part], wsem.at[1, k])

    loop(chunks, lambda k: up_copy(k).start())
    loop(chunks, lambda k: down_copy(k).start())

    small[0].wait()
    small[1].wait()
    write_t[...] = write_v[...].T
    read_t[...] = read_v[...].T
    diagonal = lax.broadcasted_iota(jnp.int32, (1, states, states), 1) == lax.broadcasted_iota(
        jnp.int32, (1, states, states), 2
    )

    def spread(n):
        part = pl.ds(pl.multiple_of(n * STEPS, STEPS), STEPS)
        for source, wide in ((write_t, wb_v), (read_t, rb_v)):
            rows = jnp.broadcast_to(source[part, :][:, None, :], (STEPS, states, states))
            picked = jnp.sum(jnp.where(diagonal, rows, 0.0), axis=2, keepdims=True)
            wide[part] = jnp.broadcast_to(picked, (STEPS, states, 128))

    loop(tokens // STEPS, spread)
    small[2].wait()
    rate2_v[...] = rates_v[...] * (-LOG2E)
    small[3].wait()
    small[4].wait()

    def widen(n):
        part = pl.ds(pl.multiple_of(n * STEPS, STEPS), STEPS)
        steps = step_v[part, :].astype(F32)
        dt_f[part, :] = steps
        u_f[part, :] = steps * x_v[part, :].astype(F32)

    loop(tokens // STEPS, widen)
    copies = channels // 128

    def advance(h, t, rate2):
        decay = jnp.exp2(dt_f[pl.ds(t, 1), :] * rate2)
        push = u_f[pl.ds(t, 1), :] * jnp.concatenate([wb_v[t]] * copies, axis=1)
        return decay * h + push

    def first(n, carry):
        h, total = carry
        rate2 = rate2_v[...]
        for r in range(STEPS):
            h = advance(h, n * STEPS + r, rate2)
        part = pl.ds(pl.multiple_of(n * STEPS, STEPS), STEPS)
        return h, total + jnp.sum(dt_f[part, :], axis=0, keepdims=True)

    h, total = lax.fori_loop(
        0,
        tokens // STEPS,
        first,
        (jnp.zeros((states, channels), F32), jnp.zeros((1, channels), F32)),
    )
    hsend[...] = h.astype(BF16)
    folded = jnp.concatenate([total[:, q * 128 : (q + 1) * 128] for q in range(copies)], axis=0)
    tsend[...] = jnp.concatenate([folded] * (8 // copies), axis=0)
    meta_v[...] = jnp.zeros_like(meta_v)
    small[9].wait()
    small[10].wait()
    meta_v[0:2, 0:mine] = ids_v[...].astype(F32)
    meta_v[2:4, 0:mine] = pairgate_v[...].astype(F32)

    wide = width // parts
    hold = parts // 2
    pack = hold * CAP
    stacked = hold * mine
    places = nexp * pack
    lanes = lax.broadcasted_iota(jnp.int32, (mine, 128), 1)
    square = lax.broadcasted_iota(jnp.int32, (mine, mine), 0) == lax.broadcasted_iota(
        jnp.int32, (mine, mine), 1
    )
    earlier = (
        lax.broadcasted_iota(jnp.int32, (mine, mine), 0)
        > lax.broadcasted_iota(jnp.int32, (mine, mine), 1)
    ).astype(F32)
    column = lax.broadcasted_iota(jnp.int32, (stacked, places), 1)
    row = lax.broadcasted_iota(jnp.int32, (stacked, places), 0)
    column_slot = lax.div(column, pack) * CAP + lax.rem(column, CAP)
    same_part = lax.rem(lax.div(column, CAP), hold) == lax.div(row, mine)
    slot_v[...] = jnp.where(same_part, column_slot, -1)

    source = lax.broadcasted_iota(jnp.int32, (places, places), 1)
    target = lax.broadcasted_iota(jnp.int32, (places, places), 0)

    def by_part(index):
        return (
            lax.rem(lax.div(index, CAP), hold) * slots
            + lax.div(index, pack) * CAP
            + lax.rem(index, CAP)
        )

    order_v[0] = (by_part(source) == target).astype(F32).astype(BF16)
    order_v[1] = (by_part(target) == source).astype(F32).astype(BF16)

    pl.semaphore_wait(barrier, nctx - 1 + 2 * (nx - 1))

    def state_copies(k):
        device = (lax.rem(i + k, nctx), j)
        return (
            remote(tsend, trecv.at[i], hs_sem.at[0, k], hr_sem.at[0, i], device),
            remote(hsend, hrecv.at[i], hs_sem.at[1, k], hr_sem.at[1, i], device),
        )

    for k in range(1, nctx):

        @pl.when(i + k < nctx)
        def _():
            for copy in state_copies(k):
                copy.start()

    def drain_states():
        for k in range(1, nctx):

            @pl.when(i + k < nctx)
            def _():
                for copy in state_copies(k):
                    copy.wait_send()

    sent = [drain_states]

    def meta_copy(k):
        return remote(
            meta_v, metas.at[z], mt_sem.at[0, k], mt_sem.at[1, z], at_z(z_next(k))
        )

    small[11].wait()
    swap = remote(w_v.at[c], w_v.at[c], wswap.at[0], wswap.at[1], partner)
    swap.start()
    sent.append(swap.wait_send)

    h_v[...] = jnp.zeros_like(h_v)
    for k in range(nctx - 1):

        @pl.when(k < i)
        def _():
            remote(tsend, trecv.at[k], hs_sem.at[0, 0], hr_sem.at[0, k], partner).wait_recv()
            remote(hsend, hrecv.at[k], hs_sem.at[1, 0], hr_sem.at[1, k], partner).wait_recv()
            passed = jnp.concatenate([trecv[k, q : q + 1, :] for q in range(copies)], axis=1)
            h_v[...] = jnp.exp2(rate2_v[...] * passed) * h_v[...] + hrecv[k].astype(F32)

    for k in range(1, nz):
        meta_copy(k).start()
    metas[z] = meta_v[...]
    sent.append(lambda: [meta_copy(k).wait_send() for k in range(1, nz)])

    small[5].wait()
    small[6].wait()

    def second(n, h):
        part = pl.ds(pl.multiple_of(n * STEPS, STEPS), STEPS)
        rate2 = rate2_v[...]
        reads = []
        for r in range(STEPS):
            t = n * STEPS + r
            h = advance(h, t, rate2)
            seen = h * jnp.concatenate([rb_v[t]] * copies, axis=1)
            reads.append(jnp.sum(seen, axis=0, keepdims=True))
        readout = jnp.concatenate(reads, axis=0)
        readout = readout + skip_v[...] * x_v[part, :].astype(F32)
        gate = gate_v[part, :].astype(F32)
        mixed_v[z, part, :] = (readout * (gate / (1.0 + jnp.exp(-gate)))).astype(BF16)
        return h

    reach = (1, nz - 1) if nz > 2 else (1,)
    beyond = tuple(range(2, nz - 1))

    def mixed_copy(n, k):
        part = mixed_v.at[z, n * (tokens // 2) : (n + 1) * (tokens // 2)]
        return remote(part, part, ms_sem.at[n, k], mr_sem.at[n, z], at_z(z_next(k)))

    def mixed_arrive(zz):
        for n in range(2):
            part = mixed_v.at[zz, n * (tokens // 2) : (n + 1) * (tokens // 2)]
            remote(part, part, ms_sem.at[n, 0], mr_sem.at[n, zz], partner).wait_recv()

    turns = tokens // STEPS // 2
    h = h_v[...]
    for n in range(2):
        h = lax.fori_loop(n * turns, (n + 1) * turns, second, h)
        for k in reach:
            mixed_copy(n, k).start()
    for n in range(2):
        for k in beyond:
            mixed_copy(n, k).start()
    sent.append(lambda: [mixed_copy(n, k).wait_send() for k in reach + beyond for n in range(2)])

    swap.wait_recv()

    def line(side, n):
        return at_e(y * nx + n) if side == 0 else at_e(n * nx + x)

    def line_of(side):
        return x if side == 0 else y

    def line_next(side, k):
        return lax.rem(line_of(side) + k, nx)

    def near_copy(side, zz, k):
        n = line_next(side, k)
        return remote(
            near_send.at[side, zz, n],
            near_recv.at[side, zz, line_of(side)],
            ps_sem.at[side, zz, k],
            pr_sem.at[side, zz, line_of(side)],
            line(side, n),
        )

    def farthest_last(k):
        return k + lax.div(k, 2) * (5 - 2 * k) if nz == 4 else k

    def project(k):
        zz = z_next(farthest_last(k))

        @pl.when(k > 0)
        def _():
            mixed_arrive(zz)

        for side in range(2):
            part = jnp.dot(mixed_v[zz], w_v[side], preferred_element_type=F32)
            part = part.reshape(nx, nx, mine, block)
            if side == 0:
                part = jnp.stack(
                    [
                        jnp.concatenate([part[b, a] for b in range(nx)], axis=0)
                        for a in range(nx)
                    ]
                )
            near_send[side, zz] = part.reshape(nx, nx * mine, block).astype(BF16)
            for n in range(1, nx):
                near_copy(side, zz, n).start()
            near_recv[side, zz, line_of(side)] = near_send[side, zz, line_of(side)]

    sent.append(
        lambda: loop(
            nz,
            lambda zz: [
                near_copy(side, zz, n).wait_send() for side in range(2) for n in range(1, nx)
            ],
        )
    )

    def far_line(side, zz, n):
        if side == 0:
            return (zz * 2 + c, n * nx + x)
        return (zz * 2 + c, y * nx + n)

    def far_copy(side, zz, k):
        n = line_next(1 - side, k)
        return remote(
            far_send.at[side, zz, n],
            far_recv.at[side, z, line_of(1 - side)],
            zs_sem.at[side, zz, k],
            zr_sem.at[side, z, line_of(1 - side)],
            far_line(side, zz, n),
        )

    def far_out(k):
        zz = z_next(farthest_last(k))
        for side in range(2):
            for n in range(1, nx):
                m = line_next(side, n)
                remote(
                    near_send.at[side, zz, m],
                    near_recv.at[side, zz, m],
                    ps_sem.at[side, zz, 0],
                    pr_sem.at[side, zz, m],
                    partner,
                ).wait_recv()
            part = near_recv[side, zz, 0].astype(F32)
            for n in range(1, nx):
                part = part + near_recv[side, zz, n].astype(F32)
            part = part.reshape(nx, mine, block)
            part = jnp.concatenate([part[:, :, : block // 2], part[:, :, block // 2 :]], axis=1)
            far_send[side, zz] = part.astype(BF16)

            @pl.when(k == 0)
            def _():
                me = line_of(1 - side)
                far_recv[side, zz, me] = far_send[side, zz, me]

            @pl.when(k > 0)
            def _():
                far_copy(side, zz, 0).start()

            for n in range(1, nx):
                far_copy(side, zz, n).start()

    project(0)
    def column_of(values):
        return jnp.sum(jnp.where(square, values, 0.0), axis=1, keepdims=True)

    def tables(zz):
        meta = metas[zz]
        idents = [column_of(meta[n : n + 1, 0:mine]).astype(jnp.int32) for n in range(2)]
        hots = [(lanes == ident).astype(F32) for ident in idents]
        before = jnp.dot(earlier, hots[0] + hots[1], preferred_element_type=F32)
        table = jnp.zeros((stacked, places), F32)
        gated = jnp.zeros((stacked, places), F32)
        for n in range(2):
            rank = jnp.sum(before * hots[n], axis=1, keepdims=True).astype(jnp.int32)
            slot = jnp.concatenate([idents[n] * CAP + rank] * hold, axis=0)
            taken = jnp.where(slot_v[...] == slot, 1.0, 0.0)
            weight = column_of(meta[n + 2 : n + 3, 0:mine])
            table = table + taken
            gated = gated + taken * jnp.concatenate([weight] * hold, axis=0)
        gated_v[zz] = gated.astype(BF16)
        table_v[zz] = table.T.astype(BF16)

    tables(z)

    def other_tables(k):
        zz = z_next(k + 1)
        remote(meta_v, metas.at[zz], mt_sem.at[0, 0], mt_sem.at[1, zz], partner).wait_recv()
        tables(zz)

    loop(nz - 1, other_tables)
    far_out(0)
    loop(nz - 1, lambda k: project(k + 1))
    loop(nz - 1, lambda k: far_out(k + 1))

    def drain_far():
        for side in range(2):
            for k in range(nz):
                for n in range(0 if k else 1, nx):
                    far_copy(side, z_next(k), n).wait_send()

    sent.append(drain_far)

    def stack(wide_rows):
        return jnp.concatenate(
            [wide_rows[:, k * wide : (k + 1) * wide] for k in range(parts)], axis=0
        )

    small[7].wait()
    small[8].wait()
    res = stack(res_v[...].astype(F32))
    gain = stack(jnp.broadcast_to(gain_v[...], (mine, width)))
    for side in range(2):
        for k in range(nz):
            for n in range(0 if k else 1, nx):
                zz, m = z_next(k), line_next(1 - side, n)
                remote(
                    far_send.at[side, zz, m],
                    far_recv.at[side, zz, m],
                    zs_sem.at[side, zz, 0],
                    zr_sem.at[side, zz, m],
                    partner,
                ).wait_recv()
    summed_parts = []
    for zz in range(nz):
        for side in range(2):
            part = far_recv[side, zz, 0].astype(F32)
            for n in range(1, nx):
                part = part + far_recv[side, zz, n].astype(F32)
            summed_parts.append(part)
    stream = (res + jnp.concatenate(summed_parts, axis=0)).astype(BF16).astype(F32)
    stream_v[...] = stream
    squares = jnp.sum(stream * stream, axis=1, keepdims=True).reshape(parts, mine, 1)
    scale = lax.rsqrt(jnp.sum(squares, axis=0) / width + EPSILON)
    normed = (stream * jnp.concatenate([scale] * parts, axis=0) * gain).astype(BF16)

    nrows[z] = normed[stacked:]

    def norm_copy(k):
        return remote(nrows.at[z], nrows.at[z], ns_sem.at[k], nr_sem.at[z], at_z(z_next(k)))

    for k in range(1, nz):
        norm_copy(k).start()
    sent.append(lambda: [norm_copy(k).wait_send() for k in range(1, nz)])

    def slotted(zz, rows):
        return (
            jnp.dot(table_v[zz], rows, preferred_element_type=F32)
            .astype(BF16)
            .reshape(nexp, pack, wide)
        )

    def left_copy(k):
        e = e_next(k)
        return remote(lsend.at[e], lrecv.at[j], ls_sem.at[k], lr_sem.at[j], at_e(e))

    lsend[...] = slotted(z, normed[:stacked])
    burst(nexp - 1, lambda k: left_copy(k + 1).start())
    lrecv[j] = lsend[j]
    sent.append(lambda: loop(nexp - 1, lambda k: left_copy(k + 1).wait_send()))

    def right_copy(k):
        e = e_next(k)
        return remote(qsend.at[e], qrecv.at[j], qs_sem.at[0, k], qr_sem.at[0, j], at_e(e))

    qsend[:, 0] = slotted(z, normed[stacked:])

    def right_out():
        def right_slots(k):
            zz = z_next(k + 1)
            remote(nrows.at[zz], nrows.at[zz], ns_sem.at[0], nr_sem.at[zz], partner).wait_recv()
            qsend[:, k + 1] = slotted(zz, nrows[zz])

        burst(nz - 1, right_slots)
        burst(nexp - 1, lambda k: right_copy(k + 1).start())
        qrecv[j] = qsend[j]
        sent.append(lambda: loop(nexp - 1, lambda k: right_copy(k + 1).wait_send()))

    def left_arrive(k):
        e = e_next(k + 1)
        remote(lsend.at[e], lrecv.at[e], ls_sem.at[0], lr_sem.at[e], partner).wait_recv()

    def rows_part(zz):
        return pl.ds(pl.multiple_of(zz * slots, slots), slots)

    def arranged(rows):
        return (
            jnp.dot(order_v[0], rows.reshape(places, wide), preferred_element_type=F32)
            .astype(BF16)
            .reshape(hold, slots, wide)
        )

    def rows_copy(g, n):
        here = rows_v.at[pl.ds(g * group, group), rows_part(z)]
        return remote(here, here, xs_sem.at[g, n], xr_sem.at[g, z], at_z(z_next(n)))

    def forward_copy(g, zz):
        return remote(
            rows_v.at[pl.ds(g * group, group), rows_part(zz)],
            rows_v.at[pl.ds(g * group, group), pl.ds(pl.multiple_of(half + zz * slots, slots), slots)],
            fs_sem.at[g, zz],
            fr_sem.at[g, zz],
            partner,
        )

    def right_forward(g):
        at = pl.ds(hold + g * group, group)
        return remote(
            rows_v.at[at, pl.ds(0, half)],
            rows_v.at[at, pl.ds(half, half)],
            gs_sem.at[g],
            gr_sem.at[g],
            partner,
        )

    group = hold // 2
    burst(nexp - 1, left_arrive)
    rows_v[0:hold, rows_part(z), :] = arranged(lrecv[...])
    for g in range(2):
        for n in range(1, nz):
            rows_copy(g, n).start()
        forward_copy(g, z).start()

    right_out()

    def right_arrive():
        def one(k):
            e = e_next(k + 1)
            remote(qsend.at[e], qrecv.at[e], qs_sem.at[0, 0], qr_sem.at[0, e], partner).wait_recv()

        burst(nexp - 1, one)

    def right_rows(k):
        rows_v[hold:parts, rows_part(z_next(k)), :] = arranged(qrecv[:, k])

    tile = 512 if hidden % 512 == 0 else hidden
    tiles = hidden // tile

    def tile_columns(n):
        return pl.ds(pl.multiple_of(n * tile, tile), tile)

    def product(start, count, columns):
        rows = jnp.concatenate([rows_v[start + k] for k in range(count)], axis=1)
        weights = up_v[start * wide : (start + count) * wide, columns]
        return jnp.dot(rows, weights, preferred_element_type=F32)

    def group_arrive(g):
        for n in range(1, nz):
            zz = z_next(farthest_last(n))
            there = rows_v.at[pl.ds(g * group, group), rows_part(zz)]
            remote(there, there, xs_sem.at[g, 0], xr_sem.at[g, zz], partner).wait_recv()
            forward_copy(g, zz).start()

    def group_forwarded(g):
        for zz in range(nz):
            forward_copy(g, zz).wait_recv()

    group_arrive(0)
    loop(chunks, lambda k: up_copy(k).wait())
    group_forwarded(0)

    def lift_first(n):
        columns = tile_columns(n)
        acc_v[:, columns] = product(0, group, columns)

    for n in range(tiles):
        lift_first(n)
    group_arrive(1)
    right_arrive()
    burst(nz, right_rows)
    for g in range(2):
        right_forward(g).start()

    def drain_rows():
        for g in range(2):
            right_forward(g).wait_send()
            for n in range(1, nz):
                rows_copy(g, n).wait_send()
            for zz in range(nz):
                forward_copy(g, zz).wait_send()

    sent.append(drain_rows)
    group_forwarded(1)

    def lift_second(n):
        columns = tile_columns(n)
        acc_v[:, columns] += product(group, group, columns)

    for n in range(tiles):
        lift_second(n)
    for g in range(2):
        right_forward(g).wait_recv()

    def lift_right(n):
        columns = tile_columns(n)
        lifted = acc_v[:, columns] + product(hold, hold, columns)
        lifted_v[:, columns] = (lifted / (1.0 + jnp.exp(-lifted))).astype(BF16)

    for n in range(tiles):
        lift_right(n)
    loop(chunks, lambda k: down_copy(k).wait())

    halves = chunks // 2

    def step_of(k):
        return lax.rem(k + halves, chunks)

    def pair_copy(k):
        return remote(osend.at[k], orecv.at[k], os_sem.at[k], or_sem.at[k], partner)

    def lower(n):
        k = step_of(n)
        columns = pl.ds(pl.multiple_of(k * block, block), block)
        product = jnp.dot(lifted_v[...], down_v[:, columns], preferred_element_type=F32)
        okeep[k] = product[0:half]
        osend[k] = product[half : 2 * half].astype(BF16)
        pair_copy(k).start()

    def paired(k):
        pair_copy(k).wait_recv()
        return okeep[k] + orecv[k].astype(F32)

    def keep_right(n):
        both = paired(halves + n).astype(BF16)
        for q in range(2):
            rsum[2 * n + q] = both[:, q * wide : (q + 1) * wide].reshape(nz, slots, wide)

    def back_copy(k, n):
        zz = z_next(n)
        return remote(
            rsend.at[k, zz], rrecv.at[k, z], rs_sem.at[k, n], rr_sem.at[k, z], at_z(zz)
        )

    def send_back(k):
        rsend[k] = paired(k).astype(BF16).reshape(nz, slots, block)
        for n in range(1, nz):
            back_copy(k, n).start()
        rrecv[k, z] = rsend[k, z]

    ahead = halves // 2
    for n in range(ahead):
        lower(halves + n)
    for n in range(halves):
        lower(n)
    burst(ahead, send_back)
    burst(halves - 1, keep_right)
    lower(halves + ahead)
    keep_right(halves - 1)

    def unarranged(rows):
        return (
            jnp.dot(order_v[1], rows.reshape(places, wide), preferred_element_type=F32)
            .astype(BF16)
            .reshape(nexp, pack, wide)
        )

    def home_right_copy(k, first):
        e = e_next(k)
        which = pl.ds(1, nz - 1) if first else pl.ds(0, 1)
        n = 0 if first else 1
        return remote(
            qsend2.at[e, which],
            qrecv2.at[j, which],
            hq_sem.at[0, n, k],
            hq_sem.at[1, n, j],
            at_e(e),
        )

    def home_right(k):
        qsend2[:, k] = unarranged(rsum[:, z_next(k)])

    burst(nz - 1, lambda k: home_right(k + 1))
    burst(nexp - 1, lambda k: home_right_copy(k + 1, True).start())
    home_right(0)
    burst(nexp - 1, lambda k: home_right_copy(k + 1, False).start())
    qrecv2[j] = qsend2[j]
    sent.append(
        lambda: loop(
            nexp - 1,
            lambda k: [home_right_copy(k + 1, first).wait_send() for first in (True, False)],
        )
    )

    for n in range(halves + ahead + 1, 2 * halves):
        lower(n)
    burst(halves - ahead, lambda n: send_back(n + ahead))

    def drain_back(k):
        for n in range(1, nz):
            back_copy(k, n).wait_send()

    sent.append(lambda: loop(halves, drain_back))
    sent.append(lambda: loop(chunks, lambda k: pair_copy(k).wait_send()))

    def back_arrive(k):
        for n in range(1, nz):
            zz = z_next(n)
            remote(
                rsend.at[k, zz], rrecv.at[k, zz], rs_sem.at[k, 0], rr_sem.at[k, zz], partner
            ).wait_recv()
        total = rrecv[k, 0].astype(F32)
        for zz in range(1, nz):
            total = total + rrecv[k, zz].astype(F32)
        for q in range(2):
            lsum[2 * k + q] = total[:, q * wide : (q + 1) * wide].astype(BF16)

    burst(halves, back_arrive)
    lsend2[...] = unarranged(lsum[...])

    def home_left_copy(k):
        e = e_next(k)
        return remote(lsend2.at[e], lrecv2.at[j], hl_sem.at[0, k], hl_sem.at[1, j], at_e(e))

    burst(nexp - 1, lambda k: home_left_copy(k + 1).start())
    lrecv2[j] = lsend2[j]
    sent.append(lambda: loop(nexp - 1, lambda k: home_left_copy(k + 1).wait_send()))

    def home_right_arrive(n):
        which = pl.ds(1, nz - 1) if n == 0 else pl.ds(0, 1)

        def one(k):
            e = e_next(k + 1)
            remote(
                qsend2.at[e, which],
                qrecv2.at[e, which],
                hq_sem.at[0, n, 0],
                hq_sem.at[1, n, e],
                partner,
            ).wait_recv()

        burst(nexp - 1, one)

    home_right_arrive(0)

    def weighed(zz, rows):
        return jnp.dot(gated_v[zz], rows.reshape(places, wide), preferred_element_type=F32)

    def token_copy(k):
        zz = z_next(k)
        return remote(csend.at[zz], crecv.at[z], cs_sem.at[0, k], cs_sem.at[1, z], at_z(zz))

    for n in range(1, nz):
        k = n + n // 2 * (5 - 2 * n) if nz == 4 else n
        zz = z_next(k)
        csend[zz] = weighed(zz, qrecv2[:, k]).astype(BF16)
        token_copy(k).start()
    home_right_arrive(1)
    crecv[z] = weighed(z, qrecv2[:, 0]).astype(BF16)
    sent.append(lambda: [token_copy(k).wait_send() for k in range(1, nz)])

    def home_left_arrive(k):
        e = e_next(k + 1)
        remote(
            lsend2.at[e], lrecv2.at[e], hl_sem.at[0, 0], hl_sem.at[1, e], partner
        ).wait_recv()

    def give(first, rows):
        for k in range(hold):
            at = (0 if first else hold) + k
            out_ref[:, at * wide : (at + 1) * wide] = rows[k * mine : (k + 1) * mine].astype(BF16)

    burst(nexp - 1, home_left_arrive)
    give(True, stream_v[0:stacked] + weighed(z, lrecv2[...]))
    for k in range(1, nz):
        zz = z_next(k)
        remote(
            csend.at[zz], crecv.at[zz], cs_sem.at[0, 0], cs_sem.at[1, zz], partner
        ).wait_recv()
    total = stream_v[stacked : 2 * stacked]
    for zz in range(nz):
        total = total + crecv[zz].astype(F32)
    give(False, total)

    for drain in sent:
        drain()


def shards(nctx, nexp, *arrays):
    (
        mixer_input,
        mixer_gate,
        step_size,
        write_coeffs,
        read_coeffs,
        decay_rates,
        skip_scale,
        out_weight,
        residual_in,
        norm_gain,
        expert_ids,
        gate_weights,
        up_weight,
        down_weight,
    ) = arrays
    tokens, channels = mixer_input.shape
    states = write_coeffs.shape[1]
    mine, width = residual_in.shape
    hidden = up_weight.shape[2]
    nz = nctx // 2
    nx = math.isqrt(nexp)
    block = width // nctx
    chunks = nctx
    slots = nexp * CAP
    parts = 2 * chunks
    wide = width // parts
    hold = parts // 2
    pack = hold * CAP
    stacked = hold * mine
    places = nexp * pack
    operands = (
        mixer_input,
        mixer_gate,
        step_size,
        write_coeffs.T,
        read_coeffs.T,
        decay_rates.T,
        skip_scale.reshape(1, channels),
        out_weight,
        residual_in,
        norm_gain.reshape(1, width),
        expert_ids.T,
        gate_weights.T,
        up_weight.reshape(width, hidden),
        down_weight.reshape(hidden, width),
    )
    dma = pltpu.SemaphoreType.DMA
    scratch = [
        pltpu.VMEM((tokens, channels), BF16),
        pltpu.VMEM((tokens, channels), BF16),
        pltpu.VMEM((tokens, channels), BF16),
        pltpu.VMEM((states, tokens), F32),
        pltpu.VMEM((states, tokens), F32),
        pltpu.VMEM((states, channels), F32),
        pltpu.VMEM((1, channels), F32),
        pltpu.VMEM((mine, width), BF16),
        pltpu.VMEM((1, width), F32),
        pltpu.VMEM((2, mine), jnp.int32),
        pltpu.VMEM((2, mine), BF16),
        pltpu.VMEM((tokens, states), F32),
        pltpu.VMEM((tokens, states), F32),
        pltpu.VMEM((width, hidden), BF16),
        pltpu.VMEM((hidden, width), BF16),
        pltpu.VMEM((2, channels, block), BF16),
        pltpu.VMEM((tokens, channels), F32),
        pltpu.VMEM((tokens, channels), F32),
        pltpu.VMEM((tokens, states, 128), F32),
        pltpu.VMEM((tokens, states, 128), F32),
        pltpu.VMEM((states, channels), F32),
        pltpu.VMEM((states, channels), F32),
        pltpu.VMEM((states, channels), BF16),
        pltpu.VMEM((nctx, states, channels), BF16),
        pltpu.VMEM((8, 128), F32),
        pltpu.VMEM((nctx, 8, 128), F32),
        pltpu.VMEM((8, 128), F32),
        pltpu.VMEM((nz, 8, 128), F32),
        pltpu.VMEM((nz, tokens, channels), BF16),
        pltpu.VMEM((2, nz, nx, nx * mine, block), BF16),
        pltpu.VMEM((2, nz, nx, nx * mine, block), BF16),
        pltpu.VMEM((2, nz, nx, 2 * mine, wide), BF16),
        pltpu.VMEM((2, nz, nx, 2 * mine, wide), BF16),
        pltpu.VMEM((parts * mine, wide), F32),
        pltpu.VMEM((nz, places, stacked), BF16),
        pltpu.VMEM((nz, stacked, places), BF16),
        pltpu.VMEM((2, places, places), BF16),
        pltpu.VMEM((stacked, places), jnp.int32),
        pltpu.VMEM((nz, stacked, wide), BF16),
        pltpu.VMEM((nexp, pack, wide), BF16),
        pltpu.VMEM((nexp, pack, wide), BF16),
        pltpu.VMEM((nexp, nz, pack, wide), BF16),
        pltpu.VMEM((nexp, nz, pack, wide), BF16),
        pltpu.VMEM((parts, nctx * slots, wide), BF16),
        pltpu.VMEM((nctx * slots, hidden), F32),
        pltpu.VMEM((nctx * slots, hidden), BF16),
        pltpu.VMEM((chunks, nz * slots, block), BF16),
        pltpu.VMEM((chunks, nz * slots, block), BF16),
        pltpu.VMEM((chunks, nz * slots, block), F32),
        pltpu.VMEM((hold, nz, slots, wide), BF16),
        pltpu.VMEM((hold, slots, wide), BF16),
        pltpu.VMEM((hold // 2, nz, slots, block), BF16),
        pltpu.VMEM((hold // 2, nz, slots, block), BF16),
        pltpu.VMEM((nexp, nz, pack, wide), BF16),
        pltpu.VMEM((nexp, nz, pack, wide), BF16),
        pltpu.VMEM((nexp, pack, wide), BF16),
        pltpu.VMEM((nexp, pack, wide), BF16),
        pltpu.VMEM((nz, stacked, wide), BF16),
        pltpu.VMEM((nz, stacked, wide), BF16),
        dma((12,)),
        dma((2, chunks)),
        dma((2,)),
        dma((2, nctx)),
        dma((2, nctx)),
        dma((2, nz)),
        dma((2, nz)),
        dma((2, nz, nx)),
        dma((2, nz, nx)),
        dma((2, nz, nx)),
        dma((2, nz, nx)),
        dma((2, nz)),
        dma((nz,)),
        dma((nz,)),
        dma((nexp,)),
        dma((nexp,)),
        dma((2, nexp)),
        dma((2, nexp)),
        dma((2, nz)),
        dma((2, nz)),
        dma((2, nz)),
        dma((2, nz)),
        dma((2,)),
        dma((2,)),
        dma((chunks,)),
        dma((chunks,)),
        dma((hold // 2, nz)),
        dma((hold // 2, nz)),
        dma((2, 2, nexp)),
        dma((2, nexp)),
        dma((2, nz)),
    ]
    return pl.pallas_call(
        functools.partial(kernel, nctx, nexp),
        out_shape=jax.ShapeDtypeStruct((mine, width), BF16),
        in_specs=[pl.BlockSpec(memory_space=pl.ANY)] * len(operands),
        out_specs=pl.BlockSpec(memory_space=pltpu.VMEM),
        scratch_shapes=scratch,
        compiler_params=pltpu.CompilerParams(
            collective_id=0, has_side_effects=True, vmem_limit_bytes=60 * 2**20
        ),
    )(*operands)


def solution(mesh):
    return jax.shard_map(
        functools.partial(shards, mesh.shape["ctx"], mesh.shape["exp"]),
        mesh=mesh,
        in_specs=(
            P("ctx", "exp"),
            P("ctx", "exp"),
            P("ctx", "exp"),
            P("ctx", None),
            P("ctx", None),
            P("exp", None),
            P("exp"),
            P("exp", "ctx"),
            P(("ctx", "exp"), None),
            P(),
            P(("ctx", "exp"), None),
            P(("ctx", "exp"), None),
            P("exp", None, "ctx"),
            P("exp", "ctx", None),
        ),
        out_specs=P(("ctx", "exp"), None),
        check_vma=False,
    )
```

```python
import functools
import math

import jax
import jax.numpy as jnp
from jax import lax
from jax.experimental import pallas as pl
from jax.experimental.pallas import tpu as pltpu
from jax.sharding import PartitionSpec as P

MESH = pl.DeviceIdType.MESH
CAP = 2
EPSILON = 1e-05
LOG2E = math.log2(math.e)
F32 = jnp.float32
BF16 = jnp.bfloat16
STEPS = 16


def remote(src, dst, send_sem, recv_sem, device):
    return pltpu.make_async_remote_copy(
        src_ref=src,
        dst_ref=dst,
        send_sem=send_sem,
        recv_sem=recv_sem,
        device_id=device,
        device_id_type=MESH,
    )


def loop(count, body):
    def step(k, carry):
        body(k)
        return carry

    lax.fori_loop(0, count, step, 0)


def burst(count, body):
    for k in range(count):
        body(k)


def kernel(
    nctx,
    nexp,
    x_hbm,
    gate_hbm,
    step_hbm,
    write_hbm,
    read_hbm,
    rates_hbm,
    skip_hbm,
    ow_hbm,
    res_hbm,
    gain_hbm,
    ids_hbm,
    pairgate_hbm,
    up_hbm,
    down_hbm,
    out_ref,
    x_v,
    gate_v,
    step_v,
    write_v,
    read_v,
    rates_v,
    skip_v,
    res_v,
    gain_v,
    ids_v,
    pairgate_v,
    write_t,
    read_t,
    up_v,
    down_v,
    w_v,
    dt_f,
    u_f,
    wb_v,
    rb_v,
    rate2_v,
    h_v,
    hsend,
    hrecv,
    tsend,
    trecv,
    meta_v,
    metas,
    mixed_v,
    near_send,
    near_recv,
    far_send,
    far_recv,
    stream_v,
    table_v,
    gated_v,
    order_v,
    slot_v,
    nrows,
    lsend,
    lrecv,
    qsend,
    qrecv,
    rows_v,
    acc_v,
    lifted_v,
    osend,
    orecv,
    okeep,
    rsum,
    lsum,
    rsend,
    rrecv,
    qsend2,
    qrecv2,
    lsend2,
    lrecv2,
    csend,
    crecv,
    lsem,
    wsem,
    wswap,
    hs_sem,
    hr_sem,
    ms_sem,
    mr_sem,
    ps_sem,
    pr_sem,
    zs_sem,
    zr_sem,
    mt_sem,
    ns_sem,
    nr_sem,
    ls_sem,
    lr_sem,
    qs_sem,
    qr_sem,
    xs_sem,
    xr_sem,
    fs_sem,
    fr_sem,
    gs_sem,
    gr_sem,
    os_sem,
    or_sem,
    rs_sem,
    rr_sem,
    hq_sem,
    hl_sem,
    cs_sem,
):
    i = lax.axis_index("ctx")
    j = lax.axis_index("exp")
    nz = nctx // 2
    z = lax.div(i, 2)
    c = lax.rem(i, 2)
    nx = math.isqrt(nexp)
    y, x = lax.div(j, nx), lax.rem(j, nx)
    partner = (z * 2 + 1 - c, j)
    tokens, channels = x_hbm.shape
    states = write_hbm.shape[0]
    mine, width = res_hbm.shape
    block = width // nctx
    hidden = up_hbm.shape[1]
    chunks = nctx
    parts = 2 * chunks
    slots = nexp * CAP
    half = nz * slots

    def at_z(zz):
        return (zz * 2 + c, j)

    def at_e(e):
        return (i, e)

    def z_next(k):
        return lax.rem(z + k, nz)

    def e_next(k):
        return lax.rem(j + k, nexp)

    barrier = pltpu.get_barrier_semaphore()

    def greet_ctx(k):
        pl.semaphore_signal(
            barrier, inc=1, device_id=(lax.rem(i + k + 1, nctx), j), device_id_type=MESH
        )

    loop(nctx - 1, greet_ctx)
    for k in range(1, nx):
        for e in (y * nx + lax.rem(x + k, nx), lax.rem(y + k, nx) * nx + x):
            pl.semaphore_signal(barrier, inc=1, device_id=at_e(e), device_id_type=MESH)

    small = [
        (write_hbm, write_v),
        (read_hbm, read_v),
        (rates_hbm, rates_v),
        (step_hbm, step_v),
        (x_hbm, x_v),
        (gate_hbm, gate_v),
        (skip_hbm, skip_v),
        (res_hbm, res_v),
        (gain_hbm, gain_v),
        (ids_hbm, ids_v),
        (pairgate_hbm, pairgate_v),
        (ow_hbm, w_v.at[c]),
    ]
    small = [
        pltpu.make_async_copy(src, dst, lsem.at[n]) for n, (src, dst) in enumerate(small)
    ]
    for copy in small:
        copy.start()

    def up_copy(k):
        part = pl.ds(pl.multiple_of(k * block, block), block)
        return pltpu.make_async_copy(up_hbm.at[part], up_v.at[part], wsem.at[0, k])

    depth = hidden // chunks

    def down_copy(k):
        part = pl.ds(pl.multiple_of(k * depth, depth), depth)
        return pltpu.make_async_copy(down_hbm.at[part], down_v.at[part], wsem.at[1, k])

    loop(chunks, lambda k: up_copy(k).start())
    loop(chunks, lambda k: down_copy(k).start())

    small[0].wait()
    small[1].wait()
    write_t[...] = write_v[...].T
    read_t[...] = read_v[...].T
    diagonal = lax.broadcasted_iota(jnp.int32, (1, states, states), 1) == lax.broadcasted_iota(
        jnp.int32, (1, states, states), 2
    )

    def spread(n):
        part = pl.ds(pl.multiple_of(n * STEPS, STEPS), STEPS)
        for source, wide in ((write_t, wb_v), (read_t, rb_v)):
            rows = jnp.broadcast_to(source[part, :][:, None, :], (STEPS, states, states))
            picked = jnp.sum(jnp.where(diagonal, rows, 0.0), axis=2, keepdims=True)
            wide[part] = jnp.broadcast_to(picked, (STEPS, states, 128))

    loop(tokens // STEPS, spread)
    small[2].wait()
    rate2_v[...] = rates_v[...] * (-LOG2E)
    small[3].wait()
    small[4].wait()

    def widen(n):
        part = pl.ds(pl.multiple_of(n * STEPS, STEPS), STEPS)
        steps = step_v[part, :].astype(F32)
        dt_f[part, :] = steps
        u_f[part, :] = steps * x_v[part, :].astype(F32)

    loop(tokens // STEPS, widen)
    copies = channels // 128

    def advance(h, t, rate2):
        decay = jnp.exp2(dt_f[pl.ds(t, 1), :] * rate2)
        push = u_f[pl.ds(t, 1), :] * jnp.concatenate([wb_v[t]] * copies, axis=1)
        return decay * h + push

    def first(n, carry):
        h, total = carry
        rate2 = rate2_v[...]
        for r in range(STEPS):
            h = advance(h, n * STEPS + r, rate2)
        part = pl.ds(pl.multiple_of(n * STEPS, STEPS), STEPS)
        return h, total + jnp.sum(dt_f[part, :], axis=0, keepdims=True)

    h, total = lax.fori_loop(
        0,
        tokens // STEPS,
        first,
        (jnp.zeros((states, channels), F32), jnp.zeros((1, channels), F32)),
    )
    hsend[...] = h.astype(BF16)
    folded = jnp.concatenate([total[:, q * 128 : (q + 1) * 128] for q in range(copies)], axis=0)
    tsend[...] = jnp.concatenate([folded] * (8 // copies), axis=0)
    meta_v[...] = jnp.zeros_like(meta_v)
    small[9].wait()
    small[10].wait()
    meta_v[0:2, 0:mine] = ids_v[...].astype(F32)
    meta_v[2:4, 0:mine] = pairgate_v[...].astype(F32)

    wide = width // parts
    hold = parts // 2
    pack = hold * CAP
    stacked = hold * mine
    places = nexp * pack
    lanes = lax.broadcasted_iota(jnp.int32, (mine, 128), 1)
    square = lax.broadcasted_iota(jnp.int32, (mine, mine), 0) == lax.broadcasted_iota(
        jnp.int32, (mine, mine), 1
    )
    earlier = (
        lax.broadcasted_iota(jnp.int32, (mine, mine), 0)
        > lax.broadcasted_iota(jnp.int32, (mine, mine), 1)
    ).astype(F32)
    column = lax.broadcasted_iota(jnp.int32, (stacked, places), 1)
    row = lax.broadcasted_iota(jnp.int32, (stacked, places), 0)
    column_slot = lax.div(column, pack) * CAP + lax.rem(column, CAP)
    same_part = lax.rem(lax.div(column, CAP), hold) == lax.div(row, mine)
    slot_v[...] = jnp.where(same_part, column_slot, -1)

    source = lax.broadcasted_iota(jnp.int32, (places, places), 1)
    target = lax.broadcasted_iota(jnp.int32, (places, places), 0)

    def by_part(index):
        return (
            lax.rem(lax.div(index, CAP), hold) * slots
            + lax.div(index, pack) * CAP
            + lax.rem(index, CAP)
        )

    order_v[0] = (by_part(source) == target).astype(F32).astype(BF16)
    order_v[1] = (by_part(target) == source).astype(F32).astype(BF16)

    pl.semaphore_wait(barrier, nctx - 1 + 2 * (nx - 1))

    def state_copies(k):
        device = (lax.rem(i + k, nctx), j)
        return (
            remote(tsend, trecv.at[i], hs_sem.at[0, k], hr_sem.at[0, i], device),
            remote(hsend, hrecv.at[i], hs_sem.at[1, k], hr_sem.at[1, i], device),
        )

    for k in range(1, nctx):

        @pl.when(i + k < nctx)
        def _():
            for copy in state_copies(k):
                copy.start()

    def drain_states():
        for k in range(1, nctx):

            @pl.when(i + k < nctx)
            def _():
                for copy in state_copies(k):
                    copy.wait_send()

    sent = [drain_states]

    def meta_copy(k):
        return remote(
            meta_v, metas.at[z], mt_sem.at[0, k], mt_sem.at[1, z], at_z(z_next(k))
        )

    small[11].wait()
    swap = remote(w_v.at[c], w_v.at[c], wswap.at[0], wswap.at[1], partner)
    swap.start()
    sent.append(swap.wait_send)

    h_v[...] = jnp.zeros_like(h_v)
    for k in range(nctx - 1):

        @pl.when(k < i)
        def _():
            remote(tsend, trecv.at[k], hs_sem.at[0, 0], hr_sem.at[0, k], partner).wait_recv()
            remote(hsend, hrecv.at[k], hs_sem.at[1, 0], hr_sem.at[1, k], partner).wait_recv()
            passed = jnp.concatenate([trecv[k, q : q + 1, :] for q in range(copies)], axis=1)
            h_v[...] = jnp.exp2(rate2_v[...] * passed) * h_v[...] + hrecv[k].astype(F32)

    for k in range(1, nz):
        meta_copy(k).start()
    metas[z] = meta_v[...]
    sent.append(lambda: [meta_copy(k).wait_send() for k in range(1, nz)])

    small[5].wait()
    small[6].wait()

    def second(n, h):
        part = pl.ds(pl.multiple_of(n * STEPS, STEPS), STEPS)
        rate2 = rate2_v[...]
        reads = []
        for r in range(STEPS):
            t = n * STEPS + r
            h = advance(h, t, rate2)
            seen = h * jnp.concatenate([rb_v[t]] * copies, axis=1)
            reads.append(jnp.sum(seen, axis=0, keepdims=True))
        readout = jnp.concatenate(reads, axis=0)
        readout = readout + skip_v[...] * x_v[part, :].astype(F32)
        gate = gate_v[part, :].astype(F32)
        mixed_v[z, part, :] = (readout * (gate / (1.0 + jnp.exp(-gate)))).astype(BF16)
        return h

    reach = (1, nz - 1) if nz > 2 else (1,)
    beyond = tuple(range(2, nz - 1))

    def mixed_copy(n, k):
        part = mixed_v.at[z, n * (tokens // 2) : (n + 1) * (tokens // 2)]
        return remote(part, part, ms_sem.at[n, k], mr_sem.at[n, z], at_z(z_next(k)))

    def mixed_arrive(zz):
        for n in range(2):
            part = mixed_v.at[zz, n * (tokens // 2) : (n + 1) * (tokens // 2)]
            remote(part, part, ms_sem.at[n, 0], mr_sem.at[n, zz], partner).wait_recv()

    turns = tokens // STEPS // 2
    h = h_v[...]
    for n in range(2):
        h = lax.fori_loop(n * turns, (n + 1) * turns, second, h)
        for k in reach:
            mixed_copy(n, k).start()
    for n in range(2):
        for k in beyond:
            mixed_copy(n, k).start()
    sent.append(lambda: [mixed_copy(n, k).wait_send() for k in reach + beyond for n in range(2)])

    swap.wait_recv()

    def line(side, n):
        return at_e(y * nx + n) if side == 0 else at_e(n * nx + x)

    def line_of(side):
        return x if side == 0 else y

    def line_next(side, k):
        return lax.rem(line_of(side) + k, nx)

    def near_copy(side, zz, k):
        n = line_next(side, k)
        return remote(
            near_send.at[side, zz, n],
            near_recv.at[side, zz, line_of(side)],
            ps_sem.at[side, zz, k],
            pr_sem.at[side, zz, line_of(side)],
            line(side, n),
        )

    def farthest_last(k):
        return k + lax.div(k, 2) * (5 - 2 * k) if nz == 4 else k

    def project(k):
        zz = z_next(farthest_last(k))

        @pl.when(k > 0)
        def _():
            mixed_arrive(zz)

        for side in range(2):
            part = jnp.dot(mixed_v[zz], w_v[side], preferred_element_type=F32)
            part = part.reshape(nx, nx, mine, block)
            if side == 0:
                part = jnp.stack(
                    [
                        jnp.concatenate([part[b, a] for b in range(nx)], axis=0)
                        for a in range(nx)
                    ]
                )
            near_send[side, zz] = part.reshape(nx, nx * mine, block).astype(BF16)
            for n in range(1, nx):
                near_copy(side, zz, n).start()
            near_recv[side, zz, line_of(side)] = near_send[side, zz, line_of(side)]

    sent.append(
        lambda: loop(
            nz,
            lambda zz: [
                near_copy(side, zz, n).wait_send() for side in range(2) for n in range(1, nx)
            ],
        )
    )

    def far_line(side, zz, n):
        if side == 0:
            return (zz * 2 + c, n * nx + x)
        return (zz * 2 + c, y * nx + n)

    def far_copy(side, zz, k):
        n = line_next(1 - side, k)
        return remote(
            far_send.at[side, zz, n],
            far_recv.at[side, z, line_of(1 - side)],
            zs_sem.at[side, zz, k],
            zr_sem.at[side, z, line_of(1 - side)],
            far_line(side, zz, n),
        )

    def far_out(k):
        zz = z_next(farthest_last(k))
        for side in range(2):
            for n in range(1, nx):
                m = line_next(side, n)
                remote(
                    near_send.at[side, zz, m],
                    near_recv.at[side, zz, m],
                    ps_sem.at[side, zz, 0],
                    pr_sem.at[side, zz, m],
                    partner,
                ).wait_recv()
            part = near_recv[side, zz, 0].astype(F32)
            for n in range(1, nx):
                part = part + near_recv[side, zz, n].astype(F32)
            part = part.reshape(nx, mine, block)
            part = jnp.concatenate([part[:, :, : block // 2], part[:, :, block // 2 :]], axis=1)
            far_send[side, zz] = part.astype(BF16)

            @pl.when(k == 0)
            def _():
                me = line_of(1 - side)
                far_recv[side, zz, me] = far_send[side, zz, me]

            @pl.when(k > 0)
            def _():
                far_copy(side, zz, 0).start()

            for n in range(1, nx):
                far_copy(side, zz, n).start()

    project(0)
    def column_of(values):
        return jnp.sum(jnp.where(square, values, 0.0), axis=1, keepdims=True)

    def tables(zz):
        meta = metas[zz]
        idents = [column_of(meta[n : n + 1, 0:mine]).astype(jnp.int32) for n in range(2)]
        hots = [(lanes == ident).astype(F32) for ident in idents]
        before = jnp.dot(earlier, hots[0] + hots[1], preferred_element_type=F32)
        table = jnp.zeros((stacked, places), F32)
        gated = jnp.zeros((stacked, places), F32)
        for n in range(2):
            rank = jnp.sum(before * hots[n], axis=1, keepdims=True).astype(jnp.int32)
            slot = jnp.concatenate([idents[n] * CAP + rank] * hold, axis=0)
            taken = jnp.where(slot_v[...] == slot, 1.0, 0.0)
            weight = column_of(meta[n + 2 : n + 3, 0:mine])
            table = table + taken
            gated = gated + taken * jnp.concatenate([weight] * hold, axis=0)
        gated_v[zz] = gated.astype(BF16)
        table_v[zz] = table.T.astype(BF16)

    tables(z)

    def other_tables(k):
        zz = z_next(k + 1)
        remote(meta_v, metas.at[zz], mt_sem.at[0, 0], mt_sem.at[1, zz], partner).wait_recv()
        tables(zz)

    loop(nz - 1, other_tables)
    far_out(0)
    loop(nz - 1, lambda k: project(k + 1))
    loop(nz - 1, lambda k: far_out(k + 1))

    def drain_far():
        for side in range(2):
            for k in range(nz):
                for n in range(0 if k else 1, nx):
                    far_copy(side, z_next(k), n).wait_send()

    sent.append(drain_far)

    def stack(wide_rows):
        return jnp.concatenate(
            [wide_rows[:, k * wide : (k + 1) * wide] for k in range(parts)], axis=0
        )

    small[7].wait()
    small[8].wait()
    res = stack(res_v[...].astype(F32))
    gain = stack(jnp.broadcast_to(gain_v[...], (mine, width)))
    for side in range(2):
        for k in range(nz):
            for n in range(0 if k else 1, nx):
                zz, m = z_next(k), line_next(1 - side, n)
                remote(
                    far_send.at[side, zz, m],
                    far_recv.at[side, zz, m],
                    zs_sem.at[side, zz, 0],
                    zr_sem.at[side, zz, m],
                    partner,
                ).wait_recv()
    summed_parts = []
    for zz in range(nz):
        for side in range(2):
            part = far_recv[side, zz, 0].astype(F32)
            for n in range(1, nx):
                part = part + far_recv[side, zz, n].astype(F32)
            summed_parts.append(part)
    stream = (res + jnp.concatenate(summed_parts, axis=0)).astype(BF16).astype(F32)
    stream_v[...] = stream
    squares = jnp.sum(stream * stream, axis=1, keepdims=True).reshape(parts, mine, 1)
    scale = lax.rsqrt(jnp.sum(squares, axis=0) / width + EPSILON)
    normed = (stream * jnp.concatenate([scale] * parts, axis=0) * gain).astype(BF16)

    nrows[z] = normed[stacked:]

    def norm_copy(k):
        return remote(nrows.at[z], nrows.at[z], ns_sem.at[k], nr_sem.at[z], at_z(z_next(k)))

    for k in range(1, nz):
        norm_copy(k).start()
    sent.append(lambda: [norm_copy(k).wait_send() for k in range(1, nz)])

    def slotted(zz, rows):
        return (
            jnp.dot(table_v[zz], rows, preferred_element_type=F32)
            .astype(BF16)
            .reshape(nexp, pack, wide)
        )

    def left_copy(k):
        e = e_next(k)
        return remote(lsend.at[e], lrecv.at[j], ls_sem.at[k], lr_sem.at[j], at_e(e))

    lsend[...] = slotted(z, normed[:stacked])
    burst(nexp - 1, lambda k: left_copy(k + 1).start())
    lrecv[j] = lsend[j]
    sent.append(lambda: loop(nexp - 1, lambda k: left_copy(k + 1).wait_send()))

    def right_copy(k):
        e = e_next(k)
        return remote(qsend.at[e], qrecv.at[j], qs_sem.at[0, k], qr_sem.at[0, j], at_e(e))

    qsend[:, 0] = slotted(z, normed[stacked:])

    def right_out():
        def right_slots(k):
            zz = z_next(k + 1)
            remote(nrows.at[zz], nrows.at[zz], ns_sem.at[0], nr_sem.at[zz], partner).wait_recv()
            qsend[:, k + 1] = slotted(zz, nrows[zz])

        burst(nz - 1, right_slots)
        burst(nexp - 1, lambda k: right_copy(k + 1).start())
        qrecv[j] = qsend[j]
        sent.append(lambda: loop(nexp - 1, lambda k: right_copy(k + 1).wait_send()))

    def left_arrive(k):
        e = e_next(k + 1)
        remote(lsend.at[e], lrecv.at[e], ls_sem.at[0], lr_sem.at[e], partner).wait_recv()

    def rows_part(zz):
        return pl.ds(pl.multiple_of(zz * slots, slots), slots)

    def arranged(rows):
        return (
            jnp.dot(order_v[0], rows.reshape(places, wide), preferred_element_type=F32)
            .astype(BF16)
            .reshape(hold, slots, wide)
        )

    def rows_copy(g, n):
        here = rows_v.at[pl.ds(g * group, group), rows_part(z)]
        return remote(here, here, xs_sem.at[g, n], xr_sem.at[g, z], at_z(z_next(n)))

    def forward_copy(g, zz):
        return remote(
            rows_v.at[pl.ds(g * group, group), rows_part(zz)],
            rows_v.at[pl.ds(g * group, group), pl.ds(pl.multiple_of(half + zz * slots, slots), slots)],
            fs_sem.at[g, zz],
            fr_sem.at[g, zz],
            partner,
        )

    def right_forward(g):
        at = pl.ds(hold + g * group, group)
        return remote(
            rows_v.at[at, pl.ds(0, half)],
            rows_v.at[at, pl.ds(half, half)],
            gs_sem.at[g],
            gr_sem.at[g],
            partner,
        )

    group = hold // 2
    burst(nexp - 1, left_arrive)
    rows_v[0:hold, rows_part(z), :] = arranged(lrecv[...])
    for g in range(2):
        for n in range(1, nz):
            rows_copy(g, n).start()
        forward_copy(g, z).start()

    right_out()

    def right_arrive():
        def one(k):
            e = e_next(k + 1)
            remote(qsend.at[e], qrecv.at[e], qs_sem.at[0, 0], qr_sem.at[0, e], partner).wait_recv()

        burst(nexp - 1, one)

    def right_rows(k):
        rows_v[hold:parts, rows_part(z_next(k)), :] = arranged(qrecv[:, k])

    tile = 512 if hidden % 512 == 0 else hidden
    tiles = hidden // tile

    def tile_columns(n):
        return pl.ds(pl.multiple_of(n * tile, tile), tile)

    def product(start, count, columns):
        rows = jnp.concatenate([rows_v[start + k] for k in range(count)], axis=1)
        weights = up_v[start * wide : (start + count) * wide, columns]
        return jnp.dot(rows, weights, preferred_element_type=F32)

    def group_arrive(g):
        for n in range(1, nz):
            zz = z_next(farthest_last(n))
            there = rows_v.at[pl.ds(g * group, group), rows_part(zz)]
            remote(there, there, xs_sem.at[g, 0], xr_sem.at[g, zz], partner).wait_recv()
            forward_copy(g, zz).start()

    def group_forwarded(g):
        for zz in range(nz):
            forward_copy(g, zz).wait_recv()

    group_arrive(0)
    loop(chunks, lambda k: up_copy(k).wait())
    group_forwarded(0)

    def lift_first(n):
        columns = tile_columns(n)
        acc_v[:, columns] = product(0, group, columns)

    for n in range(tiles):
        lift_first(n)
    group_arrive(1)
    right_arrive()
    burst(nz, right_rows)
    for g in range(2):
        right_forward(g).start()

    def drain_rows():
        for g in range(2):
            right_forward(g).wait_send()
            for n in range(1, nz):
                rows_copy(g, n).wait_send()
            for zz in range(nz):
                forward_copy(g, zz).wait_send()

    sent.append(drain_rows)
    group_forwarded(1)

    def lift_second(n):
        columns = tile_columns(n)
        acc_v[:, columns] += product(group, group, columns)

    for n in range(tiles):
        lift_second(n)
    for g in range(2):
        right_forward(g).wait_recv()

    def lift_right(n):
        columns = tile_columns(n)
        lifted = acc_v[:, columns] + product(hold, hold, columns)
        lifted_v[:, columns] = (lifted / (1.0 + jnp.exp(-lifted))).astype(BF16)

    for n in range(tiles):
        lift_right(n)
    loop(chunks, lambda k: down_copy(k).wait())

    halves = chunks // 2

    def step_of(k):
        return lax.rem(k + halves, chunks)

    def pair_copy(k):
        return remote(osend.at[k], orecv.at[k], os_sem.at[k], or_sem.at[k], partner)

    def lower(n):
        k = step_of(n)
        columns = pl.ds(pl.multiple_of(k * block, block), block)
        product = jnp.dot(lifted_v[...], down_v[:, columns], preferred_element_type=F32)
        okeep[k] = product[0:half]
        osend[k] = product[half : 2 * half].astype(BF16)
        pair_copy(k).start()

    def paired(k):
        pair_copy(k).wait_recv()
        return okeep[k] + orecv[k].astype(F32)

    def keep_right(n):
        both = paired(halves + n).astype(BF16)
        for q in range(2):
            rsum[2 * n + q] = both[:, q * wide : (q + 1) * wide].reshape(nz, slots, wide)

    def back_copy(k, n):
        zz = z_next(n)
        return remote(
            rsend.at[k, zz], rrecv.at[k, z], rs_sem.at[k, n], rr_sem.at[k, z], at_z(zz)
        )

    def send_back(k):
        rsend[k] = paired(k).astype(BF16).reshape(nz, slots, block)
        for n in range(1, nz):
            back_copy(k, n).start()
        rrecv[k, z] = rsend[k, z]

    ahead = halves // 2
    for n in range(ahead):
        lower(halves + n)
    for n in range(halves):
        lower(n)
    burst(ahead, send_back)
    burst(halves - 1, keep_right)
    for n in range(halves + ahead, 2 * halves):
        lower(n)
    keep_right(halves - 1)

    def unarranged(rows):
        return (
            jnp.dot(order_v[1], rows.reshape(places, wide), preferred_element_type=F32)
            .astype(BF16)
            .reshape(nexp, pack, wide)
        )

    def home_right_copy(k, first):
        e = e_next(k)
        which = pl.ds(1, nz - 1) if first else pl.ds(0, 1)
        n = 0 if first else 1
        return remote(
            qsend2.at[e, which],
            qrecv2.at[j, which],
            hq_sem.at[0, n, k],
            hq_sem.at[1, n, j],
            at_e(e),
        )

    def home_right(k):
        qsend2[:, k] = unarranged(rsum[:, z_next(k)])

    burst(nz - 1, lambda k: home_right(k + 1))
    burst(nexp - 1, lambda k: home_right_copy(k + 1, True).start())
    home_right(0)
    burst(nexp - 1, lambda k: home_right_copy(k + 1, False).start())
    qrecv2[j] = qsend2[j]
    sent.append(
        lambda: loop(
            nexp - 1,
            lambda k: [home_right_copy(k + 1, first).wait_send() for first in (True, False)],
        )
    )

    burst(halves - ahead, lambda n: send_back(n + ahead))

    def drain_back(k):
        for n in range(1, nz):
            back_copy(k, n).wait_send()

    sent.append(lambda: loop(halves, drain_back))
    sent.append(lambda: loop(chunks, lambda k: pair_copy(k).wait_send()))

    def back_arrive(k):
        for n in range(1, nz):
            zz = z_next(n)
            remote(
                rsend.at[k, zz], rrecv.at[k, zz], rs_sem.at[k, 0], rr_sem.at[k, zz], partner
            ).wait_recv()
        total = rrecv[k, 0].astype(F32)
        for zz in range(1, nz):
            total = total + rrecv[k, zz].astype(F32)
        for q in range(2):
            lsum[2 * k + q] = total[:, q * wide : (q + 1) * wide].astype(BF16)

    burst(halves, back_arrive)
    lsend2[...] = unarranged(lsum[...])

    def home_left_copy(k):
        e = e_next(k)
        return remote(lsend2.at[e], lrecv2.at[j], hl_sem.at[0, k], hl_sem.at[1, j], at_e(e))

    burst(nexp - 1, lambda k: home_left_copy(k + 1).start())
    lrecv2[j] = lsend2[j]
    sent.append(lambda: loop(nexp - 1, lambda k: home_left_copy(k + 1).wait_send()))

    def home_right_arrive(n):
        which = pl.ds(1, nz - 1) if n == 0 else pl.ds(0, 1)

        def one(k):
            e = e_next(k + 1)
            remote(
                qsend2.at[e, which],
                qrecv2.at[e, which],
                hq_sem.at[0, n, 0],
                hq_sem.at[1, n, e],
                partner,
            ).wait_recv()

        burst(nexp - 1, one)

    home_right_arrive(0)

    def weighed(zz, rows):
        return jnp.dot(gated_v[zz], rows.reshape(places, wide), preferred_element_type=F32)

    def token_copy(k):
        zz = z_next(k)
        return remote(csend.at[zz], crecv.at[z], cs_sem.at[0, k], cs_sem.at[1, z], at_z(zz))

    for n in range(1, nz):
        k = n + n // 2 * (5 - 2 * n) if nz == 4 else n
        zz = z_next(k)
        csend[zz] = weighed(zz, qrecv2[:, k]).astype(BF16)
        token_copy(k).start()
    home_right_arrive(1)
    crecv[z] = weighed(z, qrecv2[:, 0]).astype(BF16)
    sent.append(lambda: [token_copy(k).wait_send() for k in range(1, nz)])

    def home_left_arrive(k):
        e = e_next(k + 1)
        remote(
            lsend2.at[e], lrecv2.at[e], hl_sem.at[0, 0], hl_sem.at[1, e], partner
        ).wait_recv()

    def give(first, rows):
        for k in range(hold):
            at = (0 if first else hold) + k
            out_ref[:, at * wide : (at + 1) * wide] = rows[k * mine : (k + 1) * mine].astype(BF16)

    burst(nexp - 1, home_left_arrive)
    give(True, stream_v[0:stacked] + weighed(z, lrecv2[...]))
    for k in range(1, nz):
        zz = z_next(k)
        remote(
            csend.at[zz], crecv.at[zz], cs_sem.at[0, 0], cs_sem.at[1, zz], partner
        ).wait_recv()
    total = stream_v[stacked : 2 * stacked]
    for zz in range(nz):
        total = total + crecv[zz].astype(F32)
    give(False, total)

    for drain in sent:
        drain()


def shards(nctx, nexp, *arrays):
    (
        mixer_input,
        mixer_gate,
        step_size,
        write_coeffs,
        read_coeffs,
        decay_rates,
        skip_scale,
        out_weight,
        residual_in,
        norm_gain,
        expert_ids,
        gate_weights,
        up_weight,
        down_weight,
    ) = arrays
    tokens, channels = mixer_input.shape
    states = write_coeffs.shape[1]
    mine, width = residual_in.shape
    hidden = up_weight.shape[2]
    nz = nctx // 2
    nx = math.isqrt(nexp)
    block = width // nctx
    chunks = nctx
    slots = nexp * CAP
    parts = 2 * chunks
    wide = width // parts
    hold = parts // 2
    pack = hold * CAP
    stacked = hold * mine
    places = nexp * pack
    operands = (
        mixer_input,
        mixer_gate,
        step_size,
        write_coeffs.T,
        read_coeffs.T,
        decay_rates.T,
        skip_scale.reshape(1, channels),
        out_weight,
        residual_in,
        norm_gain.reshape(1, width),
        expert_ids.T,
        gate_weights.T,
        up_weight.reshape(width, hidden),
        down_weight.reshape(hidden, width),
    )
    dma = pltpu.SemaphoreType.DMA
    scratch = [
        pltpu.VMEM((tokens, channels), BF16),
        pltpu.VMEM((tokens, channels), BF16),
        pltpu.VMEM((tokens, channels), BF16),
        pltpu.VMEM((states, tokens), F32),
        pltpu.VMEM((states, tokens), F32),
        pltpu.VMEM((states, channels), F32),
        pltpu.VMEM((1, channels), F32),
        pltpu.VMEM((mine, width), BF16),
        pltpu.VMEM((1, width), F32),
        pltpu.VMEM((2, mine), jnp.int32),
        pltpu.VMEM((2, mine), BF16),
        pltpu.VMEM((tokens, states), F32),
        pltpu.VMEM((tokens, states), F32),
        pltpu.VMEM((width, hidden), BF16),
        pltpu.VMEM((hidden, width), BF16),
        pltpu.VMEM((2, channels, block), BF16),
        pltpu.VMEM((tokens, channels), F32),
        pltpu.VMEM((tokens, channels), F32),
        pltpu.VMEM((tokens, states, 128), F32),
        pltpu.VMEM((tokens, states, 128), F32),
        pltpu.VMEM((states, channels), F32),
        pltpu.VMEM((states, channels), F32),
        pltpu.VMEM((states, channels), BF16),
        pltpu.VMEM((nctx, states, channels), BF16),
        pltpu.VMEM((8, 128), F32),
        pltpu.VMEM((nctx, 8, 128), F32),
        pltpu.VMEM((8, 128), F32),
        pltpu.VMEM((nz, 8, 128), F32),
        pltpu.VMEM((nz, tokens, channels), BF16),
        pltpu.VMEM((2, nz, nx, nx * mine, block), BF16),
        pltpu.VMEM((2, nz, nx, nx * mine, block), BF16),
        pltpu.VMEM((2, nz, nx, 2 * mine, wide), BF16),
        pltpu.VMEM((2, nz, nx, 2 * mine, wide), BF16),
        pltpu.VMEM((parts * mine, wide), F32),
        pltpu.VMEM((nz, places, stacked), BF16),
        pltpu.VMEM((nz, stacked, places), BF16),
        pltpu.VMEM((2, places, places), BF16),
        pltpu.VMEM((stacked, places), jnp.int32),
        pltpu.VMEM((nz, stacked, wide), BF16),
        pltpu.VMEM((nexp, pack, wide), BF16),
        pltpu.VMEM((nexp, pack, wide), BF16),
        pltpu.VMEM((nexp, nz, pack, wide), BF16),
        pltpu.VMEM((nexp, nz, pack, wide), BF16),
        pltpu.VMEM((parts, nctx * slots, wide), BF16),
        pltpu.VMEM((nctx * slots, hidden), F32),
        pltpu.VMEM((nctx * slots, hidden), BF16),
        pltpu.VMEM((chunks, nz * slots, block), BF16),
        pltpu.VMEM((chunks, nz * slots, block), BF16),
        pltpu.VMEM((chunks, nz * slots, block), F32),
        pltpu.VMEM((hold, nz, slots, wide), BF16),
        pltpu.VMEM((hold, slots, wide), BF16),
        pltpu.VMEM((hold // 2, nz, slots, block), BF16),
        pltpu.VMEM((hold // 2, nz, slots, block), BF16),
        pltpu.VMEM((nexp, nz, pack, wide), BF16),
        pltpu.VMEM((nexp, nz, pack, wide), BF16),
        pltpu.VMEM((nexp, pack, wide), BF16),
        pltpu.VMEM((nexp, pack, wide), BF16),
        pltpu.VMEM((nz, stacked, wide), BF16),
        pltpu.VMEM((nz, stacked, wide), BF16),
        dma((12,)),
        dma((2, chunks)),
        dma((2,)),
        dma((2, nctx)),
        dma((2, nctx)),
        dma((2, nz)),
        dma((2, nz)),
        dma((2, nz, nx)),
        dma((2, nz, nx)),
        dma((2, nz, nx)),
        dma((2, nz, nx)),
        dma((2, nz)),
        dma((nz,)),
        dma((nz,)),
        dma((nexp,)),
        dma((nexp,)),
        dma((2, nexp)),
        dma((2, nexp)),
        dma((2, nz)),
        dma((2, nz)),
        dma((2, nz)),
        dma((2, nz)),
        dma((2,)),
        dma((2,)),
        dma((chunks,)),
        dma((chunks,)),
        dma((hold // 2, nz)),
        dma((hold // 2, nz)),
        dma((2, 2, nexp)),
        dma((2, nexp)),
        dma((2, nz)),
    ]
    return pl.pallas_call(
        functools.partial(kernel, nctx, nexp),
        out_shape=jax.ShapeDtypeStruct((mine, width), BF16),
        in_specs=[pl.BlockSpec(memory_space=pl.ANY)] * len(operands),
        out_specs=pl.BlockSpec(memory_space=pltpu.VMEM),
        scratch_shapes=scratch,
        compiler_params=pltpu.CompilerParams(
            collective_id=0, has_side_effects=True, vmem_limit_bytes=60 * 2**20
        ),
    )(*operands)


def solution(mesh):
    return jax.shard_map(
        functools.partial(shards, mesh.shape["ctx"], mesh.shape["exp"]),
        mesh=mesh,
        in_specs=(
            P("ctx", "exp"),
            P("ctx", "exp"),
            P("ctx", "exp"),
            P("ctx", None),
            P("ctx", None),
            P("exp", None),
            P("exp"),
            P("exp", "ctx"),
            P(("ctx", "exp"), None),
            P(),
            P(("ctx", "exp"), None),
            P(("ctx", "exp"), None),
            P("exp", None, "ctx"),
            P("exp", "ctx", None),
        ),
        out_specs=P(("ctx", "exp"), None),
        check_vma=False,
    )
```
